32 devices in a mesh: group: 2 (over x), head: 2 (over core), blk: 8 (over z, y).
Axes of the slice: x: 2, y: 2, z: 4, core: 2. Of those that a mesh axis runs over, the one named last changes fastest.
Arguments:
- patches: bfloat16 [4096, 1024], P(('group', 'head', 'blk')), parts along dimension 0, may hold values from -60 to 60
- ln_gain: float32 [1024], replicated, may hold values from 0.1 to 1.9
- w_qkv: bfloat16 [1024, 3072], replicated, may hold values from -0.21875 to 0.21875
- qk_gains: float32 [2, 1024], replicated, may hold values from 0.5 to 6
- w_out: bfloat16 [1024, 1024], replicated, may hold values from -0.1875 to 0.1875
Outputs:
- attn_out: bfloat16 [4096, 1024], P(('group', 'head', 'blk')), parts along dimension 0
The draws below stay inside these ranges and needn't reach their ends.
There are 2 independent parts, one for each index of `group`. The reference program is written for one: setup_inputs(seed, part) draws one part's arguments, and reference() takes and returns one part's arrays. A program takes and returns all parts, laid end to end along the dimension named above; an argument that names none is the same for every part. Nothing has to cross between parts.
All inputs are finite; a program needn't handle non-finite values.
Results may differ from the reference program's by a relative error of at most 0.025.
Values may be sent and summed in bfloat16 or wider, within the bound.
No kernel may reach another device: no remote copies, remote signals or barrier semaphores. Data moves between devices by JAX's collectives and lax.ppermute only.
A program may use at most 128 MiB of HBM per device.

```python
import math
import jax
import jax.numpy as jnp
from jax import lax

D = 1024
H = 16
HD = 64
TOKENS = 2048


def draw_patches(key, part):
    key_base = jax.random.fold_in(key, 11)
    base_rows = jax.random.normal(key_base, (TOKENS, D), jnp.float32)
    drawn = jnp.clip(base_rows, -6.0, 6.0)
    return drawn.astype(jnp.bfloat16)


def draw_w_qkv(key, part):
    scale_factor = D ** (-0.5)
    query_part = jnp.clip(jax.random.normal(jax.random.fold_in(key, 21), (D, D), jnp.float32), -6.0, 6.0) * scale_factor
    key_fresh = jnp.clip(jax.random.normal(jax.random.fold_in(key, 22), (D, D), jnp.float32), -6.0, 6.0) * scale_factor
    value_part = jnp.clip(jax.random.normal(jax.random.fold_in(key, 23), (D, D), jnp.float32), -6.0, 6.0) * scale_factor
    key_part = key_fresh
    return jnp.concatenate([query_part, key_part, value_part], axis=1).astype(jnp.bfloat16)


def draw_qk_gains(key, part):
    drawn = jnp.exp(jax.random.uniform(jax.random.fold_in(key, 33), (2, D), jnp.float32, math.log(0.5), math.log(2.5)))
    return drawn.astype(jnp.float32)


def scatter_about(rng, extent, spread, reach, held_as=jnp.bfloat16):
    return jnp.clip(spread * jax.random.normal(rng, extent, jnp.float32), -reach, reach).astype(held_as)


def setup_inputs(seed: int = 0, part: int = 0) -> dict:
    splits = jax.random.split(jax.random.key(seed), 6)
    part_keys = jax.random.split(jax.random.fold_in(splits[5], part), 6)
    patches = draw_patches(jax.random.fold_in(jax.random.fold_in(splits[5], part), 71), part)
    ln_gain = jnp.clip(1.0 + 0.18 * jax.random.normal(splits[1], (D,), jnp.float32), 0.1, 1.9)
    w_qkv = draw_w_qkv(jax.random.fold_in(splits[5], 71), part)
    qk_gains = draw_qk_gains(jax.random.fold_in(splits[5], 71), part)
    w_out = scatter_about(splits[4], (D, D), D ** -0.5, 0.1875)
    return {"patches": patches, "ln_gain": ln_gain, "w_qkv": w_qkv, "qk_gains": qk_gains, "w_out": w_out}


def layer_norm(patches, ln_gain):
    values_f = patches.astype(jnp.float32)
    centre = values_f - lax.optimization_barrier(jnp.mean(values_f, axis=-1, keepdims=True))
    variance = lax.optimization_barrier(jnp.mean(centre * centre, axis=-1, keepdims=True))
    return (centre * lax.rsqrt(variance + 1e-05) * ln_gain).astype(jnp.bfloat16)

def head_norm(columns, gain_vector, head_count):
    row_count = columns.shape[0]
    shaped = columns.reshape(row_count, head_count, HD)
    square_mean = lax.optimization_barrier(jnp.mean(shaped * shaped, axis=-1, keepdims=True))
    scaled = shaped * lax.rsqrt(square_mean + 1e-06) * gain_vector.reshape(head_count, HD)
    return scaled.astype(jnp.bfloat16).reshape(row_count, head_count * HD)

def reference(patches, ln_gain, w_qkv, qk_gains, w_out):
    normed = layer_norm(patches, ln_gain)
    projected = jnp.dot(normed, w_qkv, preferred_element_type=jnp.float32)
    query = head_norm(projected[:, :D], qk_gains[0], H)
    key_rows = head_norm(projected[:, D:2 * D], qk_gains[1], H)
    value_rows = projected[:, 2 * D:].astype(jnp.bfloat16)
    seq_count = patches.shape[0]
    block_rows = 512 if seq_count % 512 == 0 else seq_count
    score_scale = HD ** (-0.5)

    def one_head(triple):
        query_head, key_head, value_head = triple
        query_blocks = query_head.reshape(seq_count // block_rows, block_rows, HD)

        def one_block(query_block):
            scores = jnp.dot(query_block, key_head.T, preferred_element_type=jnp.float32) * score_scale
            row_max = lax.optimization_barrier(jnp.max(scores, axis=-1, keepdims=True))
            exponent = jnp.exp(scores - row_max)
            totals = lax.optimization_barrier(jnp.sum(exponent, axis=-1, keepdims=True))
            summed = jnp.dot(exponent.astype(jnp.bfloat16), value_head, preferred_element_type=jnp.float32)
            return (summed / totals).astype(jnp.bfloat16)
        return lax.map(one_block, query_blocks).reshape(seq_count, HD)

    def by_head(rows_matrix):
        return jnp.transpose(rows_matrix.reshape(seq_count, H, HD), (1, 0, 2))
    attended = lax.map(one_head, (by_head(query), by_head(key_rows), by_head(value_rows)))
    attended = jnp.transpose(attended, (1, 0, 2)).reshape(seq_count, D)
    return jnp.dot(attended, w_out, preferred_element_type=jnp.float32).astype(jnp.bfloat16)
```

```python
import functools

import jax
import jax.numpy as jnp
from jax import lax
from jax.experimental import pallas as pl
from jax.experimental.pallas import tpu as pltpu
from jax.sharding import PartitionSpec as P

H = 16
HD = 64
PAIR = 2 * HD
F32 = jnp.float32
BF16 = jnp.bfloat16
LOW = -1e30
VMEM = pl.BlockSpec(memory_space=pltpu.VMEM)


def ring_order(mesh):
    axis = mesh.axis_names.index("blk")
    along = mesh.devices
    for other in reversed(range(along.ndim)):
        if other != axis:
            along = along.take(0, axis=other)
    count = along.shape[0]
    coords = [getattr(device, "coords", None) for device in along]
    if any(c is None for c in coords):
        return list(range(count))
    place = {tuple(c): i for i, c in enumerate(coords)}
    varying = [a for a in range(3) if len({c[a] for c in place}) > 1]
    if len(place) != count or len(varying) != 2:
        return list(range(count))
    short, long = sorted(varying, key=lambda a: len({c[a] for c in place}))
    columns = sorted({c[short] for c in place})
    if len(columns) != 2:
        return list(range(count))
    up = sorted((c for c in place if c[short] == columns[0]), key=lambda c: c[long])
    down = sorted((c for c in place if c[short] == columns[1]), key=lambda c: -c[long])
    return [place[c] for c in up + down]


def normalise(x_ref, gain_ref):
    values = x_ref[...].astype(F32)
    centre = values - jnp.mean(values, axis=-1, keepdims=True)
    variance = jnp.mean(centre * centre, axis=-1, keepdims=True)
    return (centre * lax.rsqrt(variance + 1e-05) * gain_ref[...]).astype(BF16)


def head_scale(columns):
    squares = columns * columns
    high = squares.astype(BF16)
    low = (squares - high.astype(F32)).astype(BF16)
    width = 256
    row = lax.broadcasted_iota(jnp.int32, (width, width), 0) // HD
    column = lax.broadcasted_iota(jnp.int32, (width, width), 1) // HD
    same_head = jnp.where(row == column, 1.0, 0.0).astype(BF16)
    sums = [
        jnp.dot(part[:, at : at + width], same_head, preferred_element_type=F32)
        for at in range(0, columns.shape[1], width)
        for part in (high, low)
    ]
    total = jnp.concatenate([a + b for a, b in zip(sums[0::2], sums[1::2])], axis=1)
    return lax.rsqrt(total * (1.0 / HD) + 1e-06)


def query_kernel(own_ref, sibling_ref, gain_ref, wq_ref, gq_ref, out_ref):
    rows = own_ref.shape[0]
    for i, x_ref in enumerate((own_ref, sibling_ref)):
        projected = jnp.dot(normalise(x_ref, gain_ref), wq_ref[...], preferred_element_type=F32)
        query = (projected * head_scale(projected) * gq_ref[...]).astype(BF16).astype(F32)
        out_ref[:, i * rows : (i + 1) * rows] = (query * (HD**-0.5)).T.astype(BF16)


def absorb(first, last, x_ref, gain_ref, wkv_ref, gk_ref, q_ref, *refs):
    if first:
        outs = refs
    else:
        (max_ref, sum_ref, acc_ref), outs = refs[:3], refs[3:]
    width = H * HD
    projected = jnp.dot(normalise(x_ref, gain_ref), wkv_ref[...], preferred_element_type=F32)
    keys = projected[:, :width]
    keys = (keys * head_scale(keys) * gk_ref[...]).astype(BF16)
    values = projected[:, width:].T.astype(BF16)
    queries = q_ref.shape[1]
    zeros = jnp.zeros((HD, queries), BF16)
    for h in range(H):
        at = h * HD
        pair = (h // 2) * PAIR
        query = q_ref[at : at + HD, :]
        query = jnp.concatenate([query, zeros] if h % 2 == 0 else [zeros, query], axis=0)
        scores = jnp.dot(keys[:, pair : pair + PAIR], query, preferred_element_type=F32)
        new_max = jnp.max(scores, axis=0, keepdims=True)
        if not first:
            old_max = max_ref[h : h + 1, :]
            new_max = jnp.maximum(new_max, old_max)
        exponent = jnp.exp(scores - new_max)
        total = jnp.sum(exponent, axis=0, keepdims=True)
        added = jnp.dot(values[at : at + HD, :], exponent.astype(BF16), preferred_element_type=F32)
        if not first:
            shrink = jnp.exp(old_max - new_max)
            total = total + sum_ref[h : h + 1, :] * shrink
            added = added + acc_ref[at : at + HD, :] * shrink
        if last:
            keep_ref, send_ref = outs
            half = queries // 2
            for ref, part in ((keep_ref, slice(0, half)), (send_ref, slice(half, queries))):
                ref[at : at + HD, :] = added[:, part]
                ref[width + h : width + h + 1, :] = new_max[:, part]
                ref[width + H + h : width + H + h + 1, :] = total[:, part]
        else:
            new_max_ref, new_sum_ref, new_acc_ref = outs
            new_max_ref[h : h + 1, :] = new_max
            new_sum_ref[h : h + 1, :] = total
            new_acc_ref[at : at + HD, :] = added


def finish_kernel(kept_ref, came_ref, w_ref, out_ref):
    width = H * HD
    heads = []
    for h in range(H):
        at = slice(h * HD, (h + 1) * HD)
        m, s = slice(width + h, width + h + 1), slice(width + H + h, width + H + h + 1)
        top = jnp.maximum(kept_ref[m, :], came_ref[m, :])
        mine, theirs = jnp.exp(kept_ref[m, :] - top), jnp.exp(came_ref[m, :] - top)
        total = kept_ref[s, :] * mine + came_ref[s, :] * theirs
        summed = kept_ref[at, :] * mine + came_ref[at, :] * theirs
        heads.append((summed / total).astype(BF16))
    attended = jnp.concatenate(heads, axis=0)
    out_ref[...] = lax.dot_general(
        attended, w_ref[...], (((0,), (0,)), ((), ())), preferred_element_type=F32
    ).astype(BF16)


def call(body, outs, operands, flops, exps):
    moved = sum(a.size * a.dtype.itemsize for a in (*operands, *outs))
    return pl.pallas_call(
        body,
        out_shape=outs if len(outs) > 1 else outs[0],
        in_specs=[VMEM] * len(operands),
        out_specs=[VMEM] * len(outs) if len(outs) > 1 else VMEM,
        compiler_params=pltpu.CompilerParams(vmem_limit_bytes=24 * 1024 * 1024),
        cost_estimate=pl.CostEstimate(flops=flops, bytes_accessed=moved, transcendentals=exps),
    )(*operands)


def per_device(order, patches, ln_gain, w_qkv, qk_gains, w_out):
    rows, width = patches.shape
    count = lax.axis_size("blk")
    place = {index: i for i, index in enumerate(order)}

    def ahead(index, head):
        return order[(place[index] + (1 if head == 0 else -1)) % count]

    straight = [(h * count + b, h * count + ahead(b, h)) for h in range(2) for b in range(count)]
    cross = [((1 - h) * count + b, h * count + ahead(b, h)) for h in range(2) for b in range(count)]
    axes = ("head", "blk")

    gain = ln_gain.reshape(1, width)
    w_query, w_kv = w_qkv[:, :width], w_qkv[:, width:]
    gain_query, gain_key = qk_gains[0:1], qk_gains[1:2]
    sibling = lax.ppermute(patches, "head", [(0, 1), (1, 0)])
    one = lax.ppermute(patches, axes, straight)
    two = lax.ppermute(patches, axes, cross)
    query = call(
        query_kernel,
        [jax.ShapeDtypeStruct((width, 2 * rows), BF16)],
        (patches, sibling, gain, w_query, gain_query),
        2 * 2 * rows * width * width,
        0,
    )
    state_shapes = [
        jax.ShapeDtypeStruct((H, 2 * rows), F32),
        jax.ShapeDtypeStruct((H, 2 * rows), F32),
        jax.ShapeDtypeStruct((width, 2 * rows), F32),
    ]
    last_shapes = [jax.ShapeDtypeStruct((width + 2 * H, rows), F32)] * 2
    flops = 2 * rows * width * 2 * width + 2 * 2 * rows * 2 * rows * width
    exps = H * rows * 2 * rows

    def take(block, state, last=False):
        return call(
            functools.partial(absorb, not state, last),
            last_shapes if last else state_shapes,
            (block, gain, w_kv, gain_key, query, *state),
            flops,
            exps,
        )

    state = take(patches, ())
    for turn in range(1, count // 2 + 1):
        here = one
        if turn < count // 2:
            one = lax.ppermute(one, axes, straight)
            state = take(here, state)
            here = two
            if turn < count // 2 - 1:
                two = lax.ppermute(two, axes, straight)
            state = take(here, state)
        else:
            kept, sent = take(here, state, last=True)
    came = lax.ppermute(sent, "head", [(0, 1), (1, 0)])
    return call(
        finish_kernel,
        [jax.ShapeDtypeStruct((rows, width), BF16)],
        (kept, came, w_out),
        2 * rows * width * width,
        0,
    )


def solution(mesh):
    placed = (P(("group", "head", "blk"), None), P(), P(), P(), P())
    return jax.shard_map(
        functools.partial(per_device, ring_order(mesh)),
        mesh=mesh,
        in_specs=placed,
        out_specs=P(("group", "head", "blk"), None),
        check_vma=False,
    )
```

```python
import functools

import jax
import jax.numpy as jnp
from jax import lax
from jax.experimental import pallas as pl
from jax.experimental.pallas import tpu as pltpu
from jax.sharding import PartitionSpec as P

H = 16
HD = 64
PAIR = 2 * HD
SPAN = 4 * HD
F32 = jnp.float32
BF16 = jnp.bfloat16
VMEM = pl.BlockSpec(memory_space=pltpu.VMEM)


def ring_order(mesh):
    axis = mesh.axis_names.index("blk")
    along = mesh.devices
    for other in reversed(range(along.ndim)):
        if other != axis:
            along = along.take(0, axis=other)
    count = along.shape[0]
    coords = [getattr(device, "coords", None) for device in along]
    if any(c is None for c in coords):
        return list(range(count))
    place = {tuple(c): i for i, c in enumerate(coords)}
    varying = [a for a in range(3) if len({c[a] for c in place}) > 1]
    if len(place) != count or len(varying) != 2:
        return list(range(count))
    short, long = sorted(varying, key=lambda a: len({c[a] for c in place}))
    columns = sorted({c[short] for c in place})
    if len(columns) != 2:
        return list(range(count))
    up = sorted((c for c in place if c[short] == columns[0]), key=lambda c: c[long])
    down = sorted((c for c in place if c[short] == columns[1]), key=lambda c: -c[long])
    return [place[c] for c in up + down]


def normalise(x_ref, gain_ref, out_ref):
    values = x_ref[...].astype(F32)
    centre = values - jnp.mean(values, axis=-1, keepdims=True)
    variance = jnp.mean(centre * centre, axis=-1, keepdims=True)
    out_ref[...] = (centre * lax.rsqrt(variance + 1e-05) * gain_ref[...]).astype(BF16)


def same_head():
    row = lax.broadcasted_iota(jnp.int32, (SPAN, SPAN), 0) // HD
    column = lax.broadcasted_iota(jnp.int32, (SPAN, SPAN), 1) // HD
    return jnp.where(row == column, 1.0, 0.0).astype(BF16)


def head_norm(columns, gain, ones):
    squares = jnp.dot((columns * columns).astype(BF16), ones, preferred_element_type=F32)
    return (columns * lax.rsqrt(squares * (1.0 / HD) + 1e-06) * gain).astype(BF16)


def query_kernel(own_ref, sibling_ref, w_ref, gains_ref, out_ref):
    rows, width = own_ref.shape
    ones = same_head()
    own, sibling = own_ref[...], sibling_ref[...]
    spans = [slice(at, at + SPAN) for at in range(0, width, SPAN)]
    projected = [
        (i, span, jnp.dot(block, w_ref[:, span], preferred_element_type=F32))
        for i, block in enumerate((own, sibling))
        for span in spans
    ]
    for i, span, columns in projected:
        query = head_norm(columns, gains_ref[0:1, span], ones).astype(F32) * (HD**-0.5)
        out_ref[span, i * rows : (i + 1) * rows] = query.T.astype(BF16)


def absorb(first, last, block_ref, w_ref, gains_ref, q_ref, *refs):
    if first:
        outs = refs
    else:
        (max_ref, sum_ref, acc_ref), outs = refs[:3], refs[3:]
        old_max, old_sum = max_ref[...], sum_ref[...]
    width, queries = q_ref.shape
    heads = SPAN // HD
    block = block_ref[...]
    ones = same_head()
    zeros = jnp.zeros((HD, queries), BF16)
    held = {}
    maxima, sums = [], []

    def project(i):
        for name, at in (("key", width), ("value", 2 * width)):
            span = slice(at + i * SPAN, at + (i + 1) * SPAN)
            held[name, i] = jnp.dot(block, w_ref[:, span], preferred_element_type=F32)

    def norm(i):
        span = slice(i * SPAN, (i + 1) * SPAN)
        held["key", i] = head_norm(held["key", i], gains_ref[1:2, span], ones)
        held["value", i] = held["value", i].T.astype(BF16)

    def score(i):
        keys = held.pop(("key", i))
        for j in range(heads):
            at = i * SPAN + j * HD
            pair = j // 2 * PAIR
            query = q_ref[at : at + HD, :]
            query = jnp.concatenate([query, zeros] if j % 2 == 0 else [zeros, query], axis=0)
            held["score", i, j] = jnp.dot(
                keys[:, pair : pair + PAIR], query, preferred_element_type=F32
            )

    def soften(i):
        scores = [held.pop(("score", i, j)) for j in range(heads)]
        top = jnp.concatenate([jnp.max(s, axis=0, keepdims=True) for s in scores], axis=0)
        if not first:
            before = old_max[i * heads : (i + 1) * heads]
            top = jnp.maximum(top, before)
            held["shrink", i] = jnp.exp(before - top)
        exponents = [jnp.exp(s - top[j : j + 1]) for j, s in enumerate(scores)]
        total = jnp.concatenate([jnp.sum(e, axis=0, keepdims=True) for e in exponents], axis=0)
        if not first:
            total = total + old_sum[i * heads : (i + 1) * heads] * held["shrink", i]
        maxima.append(top)
        sums.append(total)
        for j, exponent in enumerate(exponents):
            held["weight", i, j] = exponent.astype(BF16)

    def weigh(i):
        values = held.pop(("value", i))
        for j in range(heads):
            at = i * SPAN + j * HD
            added = jnp.dot(
                values[j * HD : (j + 1) * HD],
                held.pop(("weight", i, j)),
                preferred_element_type=F32,
            )
            if not first:
                added = added + acc_ref[at : at + HD, :] * held["shrink", i][j : j + 1]
            if last:
                for ref, part in zip(outs, halves):
                    ref[at : at + HD, :] = added[:, part]
            else:
                outs[2][at : at + HD, :] = added

    halves = (slice(0, queries // 2), slice(queries // 2, queries))
    stages = (project, norm, score, soften, weigh)
    for turn in range(width // SPAN + len(stages) - 1):
        for behind, stage in enumerate(stages):
            if 0 <= turn - behind < width // SPAN:
                stage(turn - behind)
    top, total = jnp.concatenate(maxima, axis=0), jnp.concatenate(sums, axis=0)
    if last:
        for ref, part in zip(outs, halves):
            ref[width : width + H, :] = top[:, part]
            ref[width + H : width + 2 * H, :] = total[:, part]
    else:
        outs[0][...] = top
        outs[1][...] = total


def finish_kernel(kept_ref, came_ref, w_ref, out_ref):
    width = H * HD
    heads = []
    for h in range(H):
        at = slice(h * HD, (h + 1) * HD)
        m, s = slice(width + h, width + h + 1), slice(width + H + h, width + H + h + 1)
        top = jnp.maximum(kept_ref[m, :], came_ref[m, :])
        mine, theirs = jnp.exp(kept_ref[m, :] - top), jnp.exp(came_ref[m, :] - top)
        total = kept_ref[s, :] * mine + came_ref[s, :] * theirs
        summed = kept_ref[at, :] * mine + came_ref[at, :] * theirs
        heads.append((summed / total).astype(BF16))
    attended = jnp.concatenate(heads, axis=0)
    out_ref[...] = lax.dot_general(
        attended, w_ref[...], (((0,), (0,)), ((), ())), preferred_element_type=F32
    ).astype(BF16)


def call(body, outs, operands, flops, exps):
    moved = sum(a.size * a.dtype.itemsize for a in (*operands, *outs))
    return pl.pallas_call(
        body,
        out_shape=outs,
        in_specs=[VMEM] * len(operands),
        out_specs=[VMEM] * len(outs),
        compiler_params=pltpu.CompilerParams(vmem_limit_bytes=24 * 1024 * 1024),
        cost_estimate=pl.CostEstimate(flops=flops, bytes_accessed=moved, transcendentals=exps),
    )(*operands)


def per_device(order, patches, ln_gain, w_qkv, qk_gains, w_out):
    rows, width = patches.shape
    count = lax.axis_size("blk")
    place = {index: i for i, index in enumerate(order)}

    def ahead(index, head):
        return order[(place[index] + (1 if head == 0 else -1)) % count]

    straight = [(h * count + b, h * count + ahead(b, h)) for h in range(2) for b in range(count)]
    cross = [((1 - h) * count + b, h * count + ahead(b, h)) for h in range(2) for b in range(count)]
    axes = ("head", "blk")

    (normed,) = call(
        normalise, [jax.ShapeDtypeStruct((rows, width), BF16)], (patches, ln_gain.reshape(1, width)), 0, 0
    )
    one = lax.ppermute(normed, axes, straight)
    two = lax.ppermute(normed, axes, cross)
    sibling = lax.ppermute(normed, "head", [(0, 1), (1, 0)])
    (query,) = call(
        query_kernel,
        [jax.ShapeDtypeStruct((width, 2 * rows), BF16)],
        (normed, sibling, w_qkv, qk_gains),
        2 * 2 * rows * width * width,
        0,
    )
    state_shapes = [
        jax.ShapeDtypeStruct((H, 2 * rows), F32),
        jax.ShapeDtypeStruct((H, 2 * rows), F32),
        jax.ShapeDtypeStruct((width, 2 * rows), F32),
    ]
    last_shapes = [jax.ShapeDtypeStruct((width + 2 * H, rows), F32)] * 2
    flops = 2 * rows * width * 2 * width + 2 * 2 * rows * 2 * rows * width
    exps = H * rows * 2 * rows

    def take(block, state, last=False):
        return call(
            functools.partial(absorb, not state, last),
            last_shapes if last else state_shapes,
            (block, w_qkv, qk_gains, query, *state),
            4 * flops,
            exps,
        )

    state = take(normed, ())
    for turn in range(1, count // 2):
        here, one = one, lax.ppermute(one, axes, straight)
        state, two = lax.optimization_barrier((take(here, state), two))
        here = two
        if turn < count // 2 - 1:
            two = lax.ppermute(two, axes, straight)
        state, one = lax.optimization_barrier((take(here, state), one))
    kept, sent = take(one, state, last=True)
    came = lax.ppermute(sent, "head", [(0, 1), (1, 0)])
    return call(
        finish_kernel,
        [jax.ShapeDtypeStruct((rows, width), BF16)],
        (kept, came, w_out),
        2 * rows * width * width,
        0,
    )[0]


def solution(mesh):
    placed = (P(("group", "head", "blk"), None), P(), P(), P(), P())
    return jax.shard_map(
        functools.partial(per_device, ring_order(mesh)),
        mesh=mesh,
        in_specs=placed,
        out_specs=P(("group", "head", "blk"), None),
        check_vma=False,
    )
```

```python
import functools

import jax
import jax.numpy as jnp
from jax import lax
from jax.experimental import pallas as pl
from jax.experimental.pallas import tpu as pltpu
from jax.sharding import PartitionSpec as P

H = 16
HD = 64
PAIR = 2 * HD
SPAN = 4 * HD
F32 = jnp.float32
BF16 = jnp.bfloat16
VMEM = pl.BlockSpec(memory_space=pltpu.VMEM)


def ring_order(mesh):
    axis = mesh.axis_names.index("blk")
    along = mesh.devices
    for other in reversed(range(along.ndim)):
        if other != axis:
            along = along.take(0, axis=other)
    count = along.shape[0]
    coords = [getattr(device, "coords", None) for device in along]
    if any(c is None for c in coords):
        return list(range(count))
    place = {tuple(c): i for i, c in enumerate(coords)}
    varying = [a for a in range(3) if len({c[a] for c in place}) > 1]
    if len(place) != count or len(varying) != 2:
        return list(range(count))
    short, long = sorted(varying, key=lambda a: len({c[a] for c in place}))
    columns = sorted({c[short] for c in place})
    if len(columns) != 2:
        return list(range(count))
    up = sorted((c for c in place if c[short] == columns[0]), key=lambda c: c[long])
    down = sorted((c for c in place if c[short] == columns[1]), key=lambda c: -c[long])
    return [place[c] for c in up + down]


def same_head_kernel(out_ref):
    row = lax.broadcasted_iota(jnp.int32, out_ref.shape, 0) // HD
    column = lax.broadcasted_iota(jnp.int32, out_ref.shape, 1) // HD
    out_ref[...] = jnp.where(row == column, 1.0, 0.0).astype(BF16)


def normalised(block, gain):
    values = block.astype(F32)
    centre = values - jnp.mean(values, axis=-1, keepdims=True)
    variance = jnp.mean(centre * centre, axis=-1, keepdims=True)
    return (centre * lax.rsqrt(variance + 1e-05) * gain).astype(BF16)


def head_norm(columns, gain, ones):
    squares = jnp.dot((columns * columns).astype(BF16), ones, preferred_element_type=F32)
    return (columns * lax.rsqrt(squares * (1.0 / HD) + 1e-06) * gain).astype(BF16)


def query_kernel(
    own_ref, sibling_ref, w_ref, gain_ref, gains_ref, ones_ref, normed_ref, query_ref
):
    rows, width = own_ref.shape
    ones = ones_ref[...]
    spans = [slice(at, at + SPAN) for at in range(0, width, SPAN)]
    own = normalised(own_ref[...], gain_ref[...])
    normed_ref[...] = own
    projected = [
        (i, span, jnp.dot(block, w_ref[:, span], preferred_element_type=F32))
        for i, block in enumerate((own, normalised(sibling_ref[...], gain_ref[...])))
        for span in spans
    ]
    for i, span, columns in projected:
        query = head_norm(columns, gains_ref[0:1, span], ones).astype(F32) * (HD**-0.5)
        query_ref[span, i * rows : (i + 1) * rows] = query.T.astype(BF16)


def absorb(first, last, raw, block_ref, w_ref, gain_ref, gains_ref, ones_ref, q_ref, *refs):
    if first:
        outs = refs
    else:
        (max_ref, sum_ref, acc_ref), outs = refs[:3], refs[3:]
        old_max, old_sum = max_ref[...], sum_ref[...]
    width, queries = q_ref.shape
    heads = SPAN // HD
    block = normalised(block_ref[...], gain_ref[...]) if raw else block_ref[...]
    ones = ones_ref[...]
    zeros = jnp.zeros((HD, queries), BF16)
    held = {}
    maxima, sums = [], []

    def project(i):
        for name, at in (("key", width), ("value", 2 * width)):
            span = slice(at + i * SPAN, at + (i + 1) * SPAN)
            held[name, i] = jnp.dot(block, w_ref[:, span], preferred_element_type=F32)

    def norm(i):
        span = slice(i * SPAN, (i + 1) * SPAN)
        held["key", i] = head_norm(held["key", i], gains_ref[1:2, span], ones)
        held["value", i] = held["value", i].T.astype(BF16)

    def score(i):
        keys = held.pop(("key", i))
        for j in range(heads):
            at = i * SPAN + j * HD
            pair = j // 2 * PAIR
            query = q_ref[at : at + HD, :]
            query = jnp.concatenate([query, zeros] if j % 2 == 0 else [zeros, query], axis=0)
            held["score", i, j] = jnp.dot(
                keys[:, pair : pair + PAIR], query, preferred_element_type=F32
            )

    def soften(i):
        scores = [held.pop(("score", i, j)) for j in range(heads)]
        top = jnp.concatenate([jnp.max(s, axis=0, keepdims=True) for s in scores], axis=0)
        if not first:
            before = old_max[i * heads : (i + 1) * heads]
            top = jnp.maximum(top, before)
            held["shrink", i] = jnp.exp(before - top)
        exponents = [jnp.exp(s - top[j : j + 1]) for j, s in enumerate(scores)]
        total = jnp.concatenate([jnp.sum(e, axis=0, keepdims=True) for e in exponents], axis=0)
        if not first:
            total = total + old_sum[i * heads : (i + 1) * heads] * held["shrink", i]
        maxima.append(top)
        sums.append(total)
        for j, exponent in enumerate(exponents):
            held["weight", i, j] = exponent.astype(BF16)

    def weigh(i):
        values = held.pop(("value", i))
        for j in range(heads):
            at = i * SPAN + j * HD
            added = jnp.dot(
                values[j * HD : (j + 1) * HD],
                held.pop(("weight", i, j)),
                preferred_element_type=F32,
            )
            if not first:
                added = added + acc_ref[at : at + HD, :] * held["shrink", i][j : j + 1]
            if last:
                for ref, part in zip(outs, halves):
                    ref[at : at + HD, :] = added[:, part]
            else:
                outs[2][at : at + HD, :] = added

    halves = (slice(0, queries // 2), slice(queries // 2, queries))
    stages = (project, norm, score, soften, weigh)
    for turn in range(width // SPAN + len(stages) - 1):
        for behind, stage in enumerate(stages):
            if 0 <= turn - behind < width // SPAN:
                stage(turn - behind)
    top, total = jnp.concatenate(maxima, axis=0), jnp.concatenate(sums, axis=0)
    if last:
        for ref, part in zip(outs, halves):
            ref[width : width + H, :] = top[:, part]
            ref[width + H : width + 2 * H, :] = total[:, part]
    else:
        outs[0][...] = top
        outs[1][...] = total


def finish_kernel(kept_ref, came_ref, w_ref, out_ref):
    width = H * HD
    heads = []
    for h in range(H):
        at = slice(h * HD, (h + 1) * HD)
        m, s = slice(width + h, width + h + 1), slice(width + H + h, width + H + h + 1)
        top = jnp.maximum(kept_ref[m, :], came_ref[m, :])
        mine, theirs = jnp.exp(kept_ref[m, :] - top), jnp.exp(came_ref[m, :] - top)
        total = kept_ref[s, :] * mine + came_ref[s, :] * theirs
        summed = kept_ref[at, :] * mine + came_ref[at, :] * theirs
        heads.append((summed / total).astype(BF16))
    attended = jnp.concatenate(heads, axis=0)
    out_ref[...] = lax.dot_general(
        attended, w_ref[...], (((0,), (0,)), ((), ())), preferred_element_type=F32
    ).astype(BF16)


def call(body, outs, operands, flops, exps=0):
    moved = sum(a.size * a.dtype.itemsize for a in (*operands, *outs))
    return pl.pallas_call(
        body,
        out_shape=outs,
        in_specs=[VMEM] * len(operands),
        out_specs=[VMEM] * len(outs),
        compiler_params=pltpu.CompilerParams(vmem_limit_bytes=24 * 1024 * 1024),
        cost_estimate=pl.CostEstimate(flops=flops, bytes_accessed=moved, transcendentals=exps),
    )(*operands)


def per_device(order, patches, ln_gain, w_qkv, qk_gains, w_out):
    rows, width = patches.shape
    count = lax.axis_size("blk")
    place = {index: i for i, index in enumerate(order)}

    def ahead(index, head):
        return order[(place[index] + (1 if head == 0 else -1)) % count]

    straight = [(h * count + b, h * count + ahead(b, h)) for h in range(2) for b in range(count)]
    cross = [((1 - h) * count + b, h * count + ahead(b, h)) for h in range(2) for b in range(count)]
    axes = ("head", "blk")

    shape = jax.ShapeDtypeStruct
    tie = lax.optimization_barrier
    (ones,) = call(same_head_kernel, [shape((SPAN, SPAN), BF16)], (), 10_000_000_000)
    one = lax.ppermute(patches, axes, straight)
    sibling = lax.ppermute(patches, "head", [(0, 1), (1, 0)])
    gain = ln_gain.reshape(1, width)
    normed, query = call(
        query_kernel,
        [shape((rows, width), BF16), shape((width, 2 * rows), BF16)],
        (patches, sibling, w_qkv, gain, qk_gains, ones),
        2 * 2 * rows * width * width,
    )
    state_shapes = [
        shape((H, 2 * rows), F32),
        shape((H, 2 * rows), F32),
        shape((width, 2 * rows), F32),
    ]
    last_shapes = [shape((width + 2 * H, rows), F32)] * 2
    flops = 2 * rows * width * 2 * width + 2 * 2 * rows * 2 * rows * width

    def take(block, state, raw=True, last=False):
        return call(
            functools.partial(absorb, not state, last, raw),
            last_shapes if last else state_shapes,
            (block, w_qkv, gain, qk_gains, ones, query, *state),
            1 * flops,
            H * rows * 2 * rows,
        )

    later, query = tie((patches, query))
    two = lax.ppermute(later, axes, cross)
    state, one = tie((take(normed, (), raw=False), one))
    for turn in range(1, count // 2):
        here_one, here_two = one, two
        one = lax.ppermute(here_one, axes, straight)
        state, here_two = tie((take(here_one, state), here_two))
        if turn < count // 2 - 1:
            two = lax.ppermute(here_two, axes, straight)
        state, one = tie((take(here_two, state), one))
    kept, sent = take(one, state, last=True)
    came = lax.ppermute(sent, "head", [(0, 1), (1, 0)])
    return call(
        finish_kernel,
        [jax.ShapeDtypeStruct((rows, width), BF16)],
        (kept, came, w_out),
        2 * rows * width * width,
    )[0]


def solution(mesh):
    placed = (P(("group", "head", "blk"), None), P(), P(), P(), P())
    return jax.shard_map(
        functools.partial(per_device, ring_order(mesh)),
        mesh=mesh,
        in_specs=placed,
        out_specs=P(("group", "head", "blk"), None),
        check_vma=False,
    )
```

```python
import functools
import math

import jax
import jax.numpy as jnp
from jax import lax
from jax.experimental import pallas as pl
from jax.experimental.pallas import tpu as pltpu
from jax.sharding import PartitionSpec as P

H = 16
HD = 64
PAIR = 2 * HD
SPAN = 4 * HD
SCALE = HD**-0.5 * math.log2(math.e)
F32 = jnp.float32
BF16 = jnp.bfloat16
VMEM = pl.BlockSpec(memory_space=pltpu.VMEM)


def ring_order(mesh):
    axis = mesh.axis_names.index("blk")
    along = mesh.devices
    for other in reversed(range(along.ndim)):
        if other != axis:
            along = along.take(0, axis=other)
    count = along.shape[0]
    coords = [getattr(device, "coords", None) for device in along]
    if any(c is None for c in coords):
        return list(range(count))
    place = {tuple(c): i for i, c in enumerate(coords)}
    varying = [a for a in range(3) if len({c[a] for c in place}) > 1]
    if len(place) != count or len(varying) != 2:
        return list(range(count))
    short, long = sorted(varying, key=lambda a: len({c[a] for c in place}))
    columns = sorted({c[short] for c in place})
    if len(columns) != 2:
        return list(range(count))
    up = sorted((c for c in place if c[short] == columns[0]), key=lambda c: c[long])
    down = sorted((c for c in place if c[short] == columns[1]), key=lambda c: -c[long])
    return [place[c] for c in up + down]


def same_head_kernel(out_ref):
    row = lax.broadcasted_iota(jnp.int32, out_ref.shape, 0) // HD
    column = lax.broadcasted_iota(jnp.int32, out_ref.shape, 1) // HD
    out_ref[...] = jnp.where(row == column, 1.0, 0.0).astype(BF16)


def normalised(block, gain):
    values = block.astype(F32)
    centre = values - jnp.mean(values, axis=-1, keepdims=True)
    variance = jnp.mean(centre * centre, axis=-1, keepdims=True)
    return (centre * lax.rsqrt(variance + 1e-05) * gain).astype(BF16)


def head_norm(columns, gain, ones):
    squares = jnp.dot((columns * columns).astype(BF16), ones, preferred_element_type=F32)
    return (columns * lax.rsqrt(squares * (1.0 / HD) + 1e-06) * gain).astype(BF16)


def query_kernel(
    own_ref, sibling_ref, w_ref, gain_ref, gains_ref, ones_ref, normed_ref, query_ref
):
    rows, width = own_ref.shape
    ones = ones_ref[...]
    spans = [slice(at, at + SPAN) for at in range(0, width, SPAN)]
    own = normalised(own_ref[...], gain_ref[...])
    normed_ref[...] = own
    projected = [
        (i, span, jnp.dot(block, w_ref[:, span], preferred_element_type=F32))
        for i, block in enumerate((own, normalised(sibling_ref[...], gain_ref[...])))
        for span in spans
    ]
    for i, span, columns in projected:
        query = head_norm(columns, gains_ref[0:1, span] * SCALE, ones)
        query_ref[span, i * rows : (i + 1) * rows] = query.astype(F32).T.astype(BF16)


def absorb(first, last, raw, block_ref, w_ref, gain_ref, gains_ref, ones_ref, q_ref, *refs):
    if first:
        outs = refs
    else:
        (max_ref, sum_ref, acc_ref), outs = refs[:3], refs[3:]
        old_max, old_sum = max_ref[...], sum_ref[...]
    width, queries = q_ref.shape
    half = queries // 2
    heads = SPAN // HD
    block = normalised(block_ref[...], gain_ref[...]) if raw else block_ref[...]
    ones = ones_ref[...]
    zeros = jnp.zeros((HD, queries), BF16)
    counts = jnp.ones((16, block.shape[0]), BF16)
    held = {}
    maxima, sums = [], []

    def project(i):
        for name, at in (("key", width), ("value", 2 * width)):
            span = slice(at + i * SPAN, at + (i + 1) * SPAN)
            held[name, i] = jnp.dot(block, w_ref[:, span], preferred_element_type=F32)

    def norm(i):
        span = slice(i * SPAN, (i + 1) * SPAN)
        held["key", i] = head_norm(held["key", i], gains_ref[1:2, span], ones)
        held["value", i] = held["value", i].T.astype(BF16)

    def score(i):
        keys = held.pop(("key", i))
        for j in range(heads):
            at = i * SPAN + j * HD
            pair = j // 2 * PAIR
            query = q_ref[at : at + HD, :]
            query = jnp.concatenate([query, zeros] if j % 2 == 0 else [zeros, query], axis=0)
            held["score", i, j] = jnp.dot(
                keys[:, pair : pair + PAIR], query, preferred_element_type=F32
            )

    def soften(i):
        scores = [held.pop(("score", i, j)) for j in range(heads)]
        top = jnp.concatenate([jnp.max(s, axis=0, keepdims=True) for s in scores], axis=0)
        if not first:
            before = old_max[i * heads : (i + 1) * heads]
            top = jnp.maximum(top, before)
            held["shrink", i] = jnp.exp2(before - top)
        exponents = [jnp.exp2(s - top[j : j + 1]) for j, s in enumerate(scores)]
        maxima.append(top)
        for j, exponent in enumerate(exponents):
            held["weight", i, j] = exponent.astype(BF16)

    def weigh(i):
        values = held.pop(("value", i))
        for j in range(heads):
            at = i * SPAN + j * HD
            added = jnp.dot(
                jnp.concatenate([values[j * HD : (j + 1) * HD], counts], axis=0),
                held.pop(("weight", i, j)),
                preferred_element_type=F32,
            )
            total, added = added[HD : HD + 1], added[:HD]
            if not first:
                shrink = held["shrink", i][j : j + 1]
                total = total + old_sum[i * heads + j : i * heads + j + 1] * shrink
                added = added + acc_ref[at : at + HD, :] * shrink
            sums.append(total)
            if last:
                for ref, part in zip(outs[:2], halves):
                    ref[at : at + HD, :] = added[:, part].astype(ref.dtype)
            else:
                outs[2][at : at + HD, :] = added

    halves = (slice(0, half), slice(half, queries))
    stages = (project, norm, score, soften, weigh)
    for turn in range(width // SPAN + len(stages) - 1):
        for behind, stage in enumerate(stages):
            if 0 <= turn - behind < width // SPAN:
                stage(turn - behind)
    top, total = jnp.concatenate(maxima, axis=0), jnp.concatenate(sums, axis=0)
    if last:
        for ref, part in zip(outs[2:], halves):
            ref[:H, :] = top[:, part]
            ref[H:, :] = total[:, part]
    else:
        outs[0][...] = top
        outs[1][...] = total


def finish_kernel(mine_ref, theirs_ref, my_state_ref, their_state_ref, w_ref, out_ref):
    width = mine_ref.shape[0]
    top = jnp.maximum(my_state_ref[:H, :], their_state_ref[:H, :])
    mine = jnp.exp2(my_state_ref[:H, :] - top)
    theirs = jnp.exp2(their_state_ref[:H, :] - top)
    total = my_state_ref[H:, :] * mine + their_state_ref[H:, :] * theirs
    mine, theirs = mine / total, theirs / total
    spans = []
    for at in range(0, width, SPAN):
        merged = [
            mine_ref[h * HD : (h + 1) * HD, :] * mine[h : h + 1]
            + theirs_ref[h * HD : (h + 1) * HD, :].astype(F32) * theirs[h : h + 1]
            for h in range(at // HD, (at + SPAN) // HD)
        ]
        spans.append(jnp.concatenate(merged, axis=0).T.astype(BF16))
    attended = jnp.concatenate(spans, axis=1)
    out_ref[...] = jnp.dot(attended, w_ref[...], preferred_element_type=F32).astype(BF16)


def call(body, outs, operands, flops, exps=0):
    moved = sum(a.size * a.dtype.itemsize for a in (*operands, *outs))
    return pl.pallas_call(
        body,
        out_shape=outs,
        in_specs=[VMEM] * len(operands),
        out_specs=[VMEM] * len(outs),
        compiler_params=pltpu.CompilerParams(vmem_limit_bytes=24 * 1024 * 1024),
        cost_estimate=pl.CostEstimate(flops=flops, bytes_accessed=moved, transcendentals=exps),
    )(*operands)


def per_device(order, patches, ln_gain, w_qkv, qk_gains, w_out):
    rows, width = patches.shape
    count = lax.axis_size("blk")
    place = {index: i for i, index in enumerate(order)}

    def onward(right_core):
        return [
            (h * count + b, (1 - h) * count + order[(place[b] + step) % count])
            for b in range(count)
            for h, step in ((right_core, 1), (1 - right_core, -1))
        ]

    hops = (onward(0), onward(1))
    axes = ("head", "blk")
    swap = [(0, 1), (1, 0)]

    shape = jax.ShapeDtypeStruct
    tie = lax.optimization_barrier
    (ones,) = call(same_head_kernel, [shape((SPAN, SPAN), BF16)], (), 10_000_000_000)
    one = lax.ppermute(patches, axes, hops[0])
    sibling = lax.ppermute(patches, "head", swap)
    gain = ln_gain.reshape(1, width)
    normed, query = call(
        query_kernel,
        [shape((rows, width), BF16), shape((width, 2 * rows), BF16)],
        (patches, sibling, w_qkv, gain, qk_gains, ones),
        2 * 2 * rows * width * width,
    )
    later, query = tie((patches, query))
    two = lax.ppermute(later, axes, hops[1])
    state_shapes = [
        shape((H, 2 * rows), F32),
        shape((H, 2 * rows), F32),
        shape((width, 2 * rows), F32),
    ]
    last_shapes = [
        shape((width, rows), F32),
        shape((width, rows), BF16),
        shape((2 * H, rows), F32),
        shape((2 * H, rows), F32),
    ]
    flops = 2 * rows * width * 2 * width + 2 * 2 * rows * 2 * rows * width

    def take(block, state, raw=True, last=False):
        return call(
            functools.partial(absorb, not state, last, raw),
            last_shapes if last else state_shapes,
            (block, w_qkv, gain, qk_gains, ones, query, *state),
            1 * flops,
            H * rows * 2 * rows,
        )

    state, one = tie((take(normed, (), raw=False), one))
    for turn in range(1, count // 2):
        here_one, here_two = one, two
        one = lax.ppermute(here_one, axes, hops[turn % 2])
        state, here_two = tie((take(here_one, state), here_two))
        if turn < count // 2 - 1:
            two = lax.ppermute(here_two, axes, hops[(turn + 1) % 2])
        state, one = tie((take(here_two, state), one))
    mine, theirs, my_state, their_state = take(one, state, last=True)
    theirs = lax.ppermute(theirs, "head", swap)
    their_state = lax.ppermute(their_state, "head", swap)
    return call(
        finish_kernel,
        [shape((rows, width), BF16)],
        (mine, theirs, my_state, their_state, w_out),
        2 * rows * width * width,
    )[0]


def solution(mesh):
    placed = (P(("group", "head", "blk"), None), P(), P(), P(), P())
    return jax.shard_map(
        functools.partial(per_device, ring_order(mesh)),
        mesh=mesh,
        in_specs=placed,
        out_specs=P(("group", "head", "blk"), None),
        check_vma=False,
    )
```

```python
import functools
import math

import jax
import jax.numpy as jnp
from jax import lax
from jax.experimental import pallas as pl
from jax.experimental.pallas import tpu as pltpu
from jax.sharding import PartitionSpec as P

H = 16
HD = 64
PAIR = 2 * HD
SPAN = 4 * HD
SCALE = HD**-0.5 * math.log2(math.e)
F32 = jnp.float32
BF16 = jnp.bfloat16
VMEM = pl.BlockSpec(memory_space=pltpu.VMEM)


def ring_order(mesh):
    axis = mesh.axis_names.index("blk")
    along = mesh.devices
    for other in reversed(range(along.ndim)):
        if other != axis:
            along = along.take(0, axis=other)
    count = along.shape[0]
    coords = [getattr(device, "coords", None) for device in along]
    if any(c is None for c in coords):
        return list(range(count))
    place = {tuple(c): i for i, c in enumerate(coords)}
    varying = [a for a in range(3) if len({c[a] for c in place}) > 1]
    if len(place) != count or len(varying) != 2:
        return list(range(count))
    short, long = sorted(varying, key=lambda a: len({c[a] for c in place}))
    columns = sorted({c[short] for c in place})
    if len(columns) != 2:
        return list(range(count))
    up = sorted((c for c in place if c[short] == columns[0]), key=lambda c: c[long])
    down = sorted((c for c in place if c[short] == columns[1]), key=lambda c: -c[long])
    return [place[c] for c in up + down]


def same_head_kernel(out_ref):
    row = lax.broadcasted_iota(jnp.int32, out_ref.shape, 0) // HD
    column = lax.broadcasted_iota(jnp.int32, out_ref.shape, 1) // HD
    out_ref[...] = jnp.where(row == column, 1.0, 0.0).astype(BF16)


def normalised(block, gain):
    values = block.astype(F32)
    centre = values - jnp.mean(values, axis=-1, keepdims=True)
    variance = jnp.mean(centre * centre, axis=-1, keepdims=True)
    return (centre * lax.rsqrt(variance + 1e-05) * gain).astype(BF16)


def head_norm(columns, gain, ones):
    squares = jnp.dot((columns * columns).astype(BF16), ones, preferred_element_type=F32)
    return (columns * lax.rsqrt(squares * (1.0 / HD) + 1e-06) * gain).astype(BF16)


def query_kernel(
    own_ref, sibling_ref, w_ref, gain_ref, gains_ref, ones_ref, normed_ref, query_ref
):
    rows, width = own_ref.shape
    ones = ones_ref[...]
    spans = [slice(at, at + SPAN) for at in range(0, width, SPAN)]
    own = normalised(own_ref[...], gain_ref[...])
    normed_ref[...] = own
    projected = [
        (i, span, jnp.dot(block, w_ref[:, span], preferred_element_type=F32))
        for i, block in enumerate((own, normalised(sibling_ref[...], gain_ref[...])))
        for span in spans
    ]
    for i, span, columns in projected:
        query = head_norm(columns, gains_ref[0:1, span] * SCALE, ones)
        query_ref[span, i * rows : (i + 1) * rows] = query.astype(F32).T.astype(BF16)


def absorb(first, last, raws, *refs):
    blocks, refs = refs[: len(raws)], refs[len(raws) :]
    w_ref, gain_ref, gains_ref, ones_ref, q_ref = refs[:5]
    if first:
        outs = refs[5:]
    else:
        (max_ref, sum_ref, acc_ref), outs = refs[5:8], refs[8:]
        old_max, old_sum = max_ref[...], sum_ref[...]
    width, queries = q_ref.shape
    half = queries // 2
    heads = SPAN // HD
    blocks = [
        normalised(ref[...], gain_ref[...]) if raw else ref[...] for ref, raw in zip(blocks, raws)
    ]
    block = jnp.concatenate(blocks, axis=0) if len(blocks) > 1 else blocks[0]
    ones = ones_ref[...]
    zeros = jnp.zeros((HD, queries), BF16)
    counts = jnp.ones((16, block.shape[0]), BF16)
    held = {}
    maxima, sums = [], []

    def project(i):
        for name, at in (("key", width), ("value", 2 * width)):
            span = slice(at + i * SPAN, at + (i + 1) * SPAN)
            held[name, i] = jnp.dot(block, w_ref[:, span], preferred_element_type=F32)

    def norm(i):
        span = slice(i * SPAN, (i + 1) * SPAN)
        held["key", i] = head_norm(held["key", i], gains_ref[1:2, span], ones)
        held["value", i] = held["value", i].T.astype(BF16)

    def score(i):
        keys = held.pop(("key", i))
        for j in range(heads):
            at = i * SPAN + j * HD
            pair = j // 2 * PAIR
            query = q_ref[at : at + HD, :]
            query = jnp.concatenate([query, zeros] if j % 2 == 0 else [zeros, query], axis=0)
            held["score", i, j] = jnp.dot(
                keys[:, pair : pair + PAIR], query, preferred_element_type=F32
            )

    def soften(i):
        scores = [held.pop(("score", i, j)) for j in range(heads)]
        top = jnp.concatenate([jnp.max(s, axis=0, keepdims=True) for s in scores], axis=0)
        if not first:
            before = old_max[i * heads : (i + 1) * heads]
            top = jnp.maximum(top, before)
            held["shrink", i] = jnp.exp2(before - top)
        exponents = [jnp.exp2(s - top[j : j + 1]) for j, s in enumerate(scores)]
        maxima.append(top)
        for j, exponent in enumerate(exponents):
            held["weight", i, j] = exponent.astype(BF16)

    def weigh(i):
        values = held.pop(("value", i))
        for j in range(heads):
            at = i * SPAN + j * HD
            added = jnp.dot(
                jnp.concatenate([values[j * HD : (j + 1) * HD], counts], axis=0),
                held.pop(("weight", i, j)),
                preferred_element_type=F32,
            )
            total, added = added[HD : HD + 1], added[:HD]
            if not first:
                shrink = held["shrink", i][j : j + 1]
                total = total + old_sum[i * heads + j : i * heads + j + 1] * shrink
                added = added + acc_ref[at : at + HD, :] * shrink
            sums.append(total)
            if last:
                for ref, part in zip(outs[:2], halves):
                    ref[at : at + HD, :] = added[:, part].astype(ref.dtype)
            else:
                outs[2][at : at + HD, :] = added

    halves = (slice(0, half), slice(half, queries))
    stages = (project, norm, score, soften, weigh)
    for turn in range(width // SPAN + len(stages) - 1):
        for behind, stage in enumerate(stages):
            if 0 <= turn - behind < width // SPAN:
                stage(turn - behind)
    top, total = jnp.concatenate(maxima, axis=0), jnp.concatenate(sums, axis=0)
    if last:
        for ref, part in zip(outs[2:], halves):
            ref[:H, :] = top[:, part]
            ref[H:, :] = total[:, part]
    else:
        outs[0][...] = top
        outs[1][...] = total


def finish_kernel(mine_ref, theirs_ref, my_state_ref, their_state_ref, w_ref, out_ref):
    width = mine_ref.shape[0]
    top = jnp.maximum(my_state_ref[:H, :], their_state_ref[:H, :])
    mine = jnp.exp2(my_state_ref[:H, :] - top)
    theirs = jnp.exp2(their_state_ref[:H, :] - top)
    total = my_state_ref[H:, :] * mine + their_state_ref[H:, :] * theirs
    mine, theirs = mine / total, theirs / total
    spans = []
    for at in range(0, width, SPAN):
        merged = [
            mine_ref[h * HD : (h + 1) * HD, :] * mine[h : h + 1]
            + theirs_ref[h * HD : (h + 1) * HD, :].astype(F32) * theirs[h : h + 1]
            for h in range(at // HD, (at + SPAN) // HD)
        ]
        spans.append(jnp.concatenate(merged, axis=0).T.astype(BF16))
    attended = jnp.concatenate(spans, axis=1)
    out_ref[...] = jnp.dot(attended, w_ref[...], preferred_element_type=F32).astype(BF16)


def call(body, outs, operands, flops, exps=0):
    moved = sum(a.size * a.dtype.itemsize for a in (*operands, *outs))
    return pl.pallas_call(
        body,
        out_shape=outs,
        in_specs=[VMEM] * len(operands),
        out_specs=[VMEM] * len(outs),
        compiler_params=pltpu.CompilerParams(vmem_limit_bytes=24 * 1024 * 1024),
        cost_estimate=pl.CostEstimate(flops=flops, bytes_accessed=moved, transcendentals=exps),
    )(*operands)


def per_device(order, patches, ln_gain, w_qkv, qk_gains, w_out):
    rows, width = patches.shape
    count = lax.axis_size("blk")
    place = {index: i for i, index in enumerate(order)}

    def onward(right_core):
        return [
            (h * count + b, (1 - h) * count + order[(place[b] + step) % count])
            for b in range(count)
            for h, step in ((right_core, 1), (1 - right_core, -1))
        ]

    hops = (onward(0), onward(1))
    axes = ("head", "blk")
    swap = [(0, 1), (1, 0)]

    shape = jax.ShapeDtypeStruct
    tie = lax.optimization_barrier
    (ones,) = call(same_head_kernel, [shape((SPAN, SPAN), BF16)], (), 10_000_000_000)
    one = lax.ppermute(patches, axes, hops[0])
    sibling = lax.ppermute(patches, "head", swap)
    gain = ln_gain.reshape(1, width)
    normed, query = call(
        query_kernel,
        [shape((rows, width), BF16), shape((width, 2 * rows), BF16)],
        (patches, sibling, w_qkv, gain, qk_gains, ones),
        2 * 2 * rows * width * width,
    )
    later, query = tie((normed, query))
    two = lax.ppermute(later, axes, hops[1])
    state_shapes = [
        shape((H, 2 * rows), F32),
        shape((H, 2 * rows), F32),
        shape((width, 2 * rows), F32),
    ]
    last_shapes = [
        shape((width, rows), F32),
        shape((width, rows), BF16),
        shape((2 * H, rows), F32),
        shape((2 * H, rows), F32),
    ]
    flops = 2 * rows * width * 2 * width + 2 * 2 * rows * 2 * rows * width

    def take(blocks, state, last=False):
        arrays, raws = zip(*blocks)
        return call(
            functools.partial(absorb, not state, last, raws),
            last_shapes if last else state_shapes,
            (*arrays, w_qkv, gain, qk_gains, ones, query, *state),
            len(blocks) * flops,
            len(blocks) * H * rows * 2 * rows,
        )

    one, query = tie((one, query))
    late, state = (normed, False), ()
    for turn in range(1, count // 2):
        here_one, here_two = one, two
        one = lax.ppermute(here_one, axes, hops[turn % 2])
        if turn < count // 2 - 1:
            state, here_two = tie((take([late], state), here_two))
            two = lax.ppermute(here_two, axes, hops[(turn + 1) % 2])
            state, one = tie((take([(here_one, True)], state), one))
            late = here_two, False
    state, here_two = tie((take([late, (here_one, True)], state), here_two))
    state, one = tie((take([(here_two, False)], state), one))
    mine, theirs, my_state, their_state = take([(one, True)], state, last=True)
    theirs = lax.ppermute(theirs, "head", swap)
    their_state = lax.ppermute(their_state, "head", swap)
    return call(
        finish_kernel,
        [shape((rows, width), BF16)],
        (mine, theirs, my_state, their_state, w_out),
        2 * rows * width * width,
    )[0]


def solution(mesh):
    placed = (P(("group", "head", "blk"), None), P(), P(), P(), P())
    return jax.shard_map(
        functools.partial(per_device, ring_order(mesh)),
        mesh=mesh,
        in_specs=placed,
        out_specs=P(("group", "head", "blk"), None),
        check_vma=False,
    )
```

```python
import functools
import math

import jax
import jax.numpy as jnp
from jax import lax
from jax.experimental import pallas as pl
from jax.experimental.pallas import tpu as pltpu
from jax.sharding import PartitionSpec as P

H = 16
HD = 64
PAIR = 2 * HD
SPAN = 4 * HD
SCALE = HD**-0.5 * math.log2(math.e)
F32 = jnp.float32
BF16 = jnp.bfloat16
VMEM = pl.BlockSpec(memory_space=pltpu.VMEM)


def ring_order(mesh):
    axis = mesh.axis_names.index("blk")
    along = mesh.devices
    for other in reversed(range(along.ndim)):
        if other != axis:
            along = along.take(0, axis=other)
    count = along.shape[0]
    coords = [getattr(device, "coords", None) for device in along]
    if any(c is None for c in coords):
        return list(range(count))
    place = {tuple(c): i for i, c in enumerate(coords)}
    varying = [a for a in range(3) if len({c[a] for c in place}) > 1]
    if len(place) != count or len(varying) != 2:
        return list(range(count))
    short, long = sorted(varying, key=lambda a: len({c[a] for c in place}))
    columns = sorted({c[short] for c in place})
    if len(columns) != 2:
        return list(range(count))
    up = sorted((c for c in place if c[short] == columns[0]), key=lambda c: c[long])
    down = sorted((c for c in place if c[short] == columns[1]), key=lambda c: -c[long])
    return [place[c] for c in up + down]


def same_head_kernel(out_ref):
    row = lax.broadcasted_iota(jnp.int32, out_ref.shape, 0) // HD
    column = lax.broadcasted_iota(jnp.int32, out_ref.shape, 1) // HD
    out_ref[...] = jnp.where(row == column, 1.0, 0.0).astype(BF16)


def normalised(block, gain):
    values = block.astype(F32)
    centre = values - jnp.mean(values, axis=-1, keepdims=True)
    variance = jnp.mean(centre * centre, axis=-1, keepdims=True)
    return (centre * lax.rsqrt(variance + 1e-05) * gain).astype(BF16)


def head_norm(columns, gain, ones):
    squares = jnp.dot((columns * columns).astype(BF16), ones, preferred_element_type=F32)
    return (columns * lax.rsqrt(squares * (1.0 / HD) + 1e-06) * gain).astype(BF16)


def normalise_kernel(own_ref, sibling_ref, gain_ref, w_ref, out_ref, other_ref):
    for ref, block_ref in ((out_ref, own_ref), (other_ref, sibling_ref)):
        ref[...] = normalised(block_ref[...], gain_ref[...])


def query_kernel(own_ref, sibling_ref, w_ref, gains_ref, ones_ref, query_ref):
    rows, width = own_ref.shape
    ones = ones_ref[...]
    spans = [slice(at, at + SPAN) for at in range(0, width, SPAN)]
    projected = [
        (i, span, jnp.dot(ref[...], w_ref[:, span], preferred_element_type=F32))
        for i, ref in enumerate((own_ref, sibling_ref))
        for span in spans
    ]
    for i, span, columns in projected:
        query = head_norm(columns, gains_ref[0:1, span] * SCALE, ones)
        query_ref[span, i * rows : (i + 1) * rows] = query.astype(F32).T.astype(BF16)


def absorb(first, last, raws, *refs):
    blocks, refs = refs[: len(raws)], refs[len(raws) :]
    w_ref, gain_ref, gains_ref, ones_ref, q_ref = refs[:5]
    if first:
        outs = refs[5:]
    else:
        (max_ref, sum_ref, acc_ref), outs = refs[5:8], refs[8:]
        old_max, old_sum = max_ref[...], sum_ref[...]
    width, queries = q_ref.shape
    half = queries // 2
    heads = SPAN // HD
    blocks = [
        normalised(ref[...], gain_ref[...]) if raw else ref[...] for ref, raw in zip(blocks, raws)
    ]
    block = jnp.concatenate(blocks, axis=0) if len(blocks) > 1 else blocks[0]
    ones = ones_ref[...]
    zeros = jnp.zeros((HD, queries), BF16)
    counts = jnp.ones((16, block.shape[0]), BF16)
    held = {}
    maxima, sums = [], []

    def project(i):
        for name, at in (("key", width), ("value", 2 * width)):
            span = slice(at + i * SPAN, at + (i + 1) * SPAN)
            held[name, i] = jnp.dot(block, w_ref[:, span], preferred_element_type=F32)

    def norm(i):
        span = slice(i * SPAN, (i + 1) * SPAN)
        held["key", i] = head_norm(held["key", i], gains_ref[1:2, span], ones)
        held["value", i] = held["value", i].T.astype(BF16)

    def score(i):
        keys = held.pop(("key", i))
        for j in range(heads):
            at = i * SPAN + j * HD
            pair = j // 2 * PAIR
            query = q_ref[at : at + HD, :]
            query = jnp.concatenate([query, zeros] if j % 2 == 0 else [zeros, query], axis=0)
            held["score", i, j] = jnp.dot(
                keys[:, pair : pair + PAIR], query, preferred_element_type=F32
            )

    def soften(i):
        scores = [held.pop(("score", i, j)) for j in range(heads)]
        top = jnp.concatenate([jnp.max(s, axis=0, keepdims=True) for s in scores], axis=0)
        if not first:
            before = old_max[i * heads : (i + 1) * heads]
            top = jnp.maximum(top, before)
            held["shrink", i] = jnp.exp2(before - top)
        exponents = [jnp.exp2(s - top[j : j + 1]) for j, s in enumerate(scores)]
        maxima.append(top)
        for j, exponent in enumerate(exponents):
            held["weight", i, j] = exponent.astype(BF16)

    def weigh(i):
        values = held.pop(("value", i))
        for j in range(heads):
            at = i * SPAN + j * HD
            added = jnp.dot(
                jnp.concatenate([values[j * HD : (j + 1) * HD], counts], axis=0),
                held.pop(("weight", i, j)),
                preferred_element_type=F32,
            )
            total, added = added[HD : HD + 1], added[:HD]
            if not first:
                shrink = held["shrink", i][j : j + 1]
                total = total + old_sum[i * heads + j : i * heads + j + 1] * shrink
                added = added + acc_ref[at : at + HD, :] * shrink
            sums.append(total)
            if last:
                for ref, part in zip(outs[:2], halves):
                    ref[at : at + HD, :] = added[:, part].astype(ref.dtype)
            else:
                outs[2][at : at + HD, :] = added

    halves = (slice(0, half), slice(half, queries))
    stages = (project, norm, score, soften, weigh)
    for turn in range(width // SPAN + len(stages) - 1):
        for behind, stage in enumerate(stages):
            if 0 <= turn - behind < width // SPAN:
                stage(turn - behind)
    top, total = jnp.concatenate(maxima, axis=0), jnp.concatenate(sums, axis=0)
    if last:
        for ref, part in zip(outs[2:], halves):
            ref[:H, :] = top[:, part]
            ref[H:, :] = total[:, part]
    else:
        outs[0][...] = top
        outs[1][...] = total


def finish_kernel(mine_ref, theirs_ref, my_state_ref, their_state_ref, w_ref, out_ref):
    width = mine_ref.shape[0]
    top = jnp.maximum(my_state_ref[:H, :], their_state_ref[:H, :])
    mine = jnp.exp2(my_state_ref[:H, :] - top)
    theirs = jnp.exp2(their_state_ref[:H, :] - top)
    total = my_state_ref[H:, :] * mine + their_state_ref[H:, :] * theirs
    mine, theirs = mine / total, theirs / total
    spans = []
    for at in range(0, width, SPAN):
        merged = [
            mine_ref[h * HD : (h + 1) * HD, :] * mine[h : h + 1]
            + theirs_ref[h * HD : (h + 1) * HD, :].astype(F32) * theirs[h : h + 1]
            for h in range(at // HD, (at + SPAN) // HD)
        ]
        spans.append(jnp.concatenate(merged, axis=0).T.astype(BF16))
    attended = jnp.concatenate(spans, axis=1)
    out_ref[...] = jnp.dot(attended, w_ref[...], preferred_element_type=F32).astype(BF16)


def call(body, outs, operands, flops, exps=0):
    moved = sum(a.size * a.dtype.itemsize for a in (*operands, *outs))
    return pl.pallas_call(
        body,
        out_shape=outs,
        in_specs=[VMEM] * len(operands),
        out_specs=[VMEM] * len(outs),
        compiler_params=pltpu.CompilerParams(vmem_limit_bytes=24 * 1024 * 1024),
        cost_estimate=pl.CostEstimate(flops=flops, bytes_accessed=moved, transcendentals=exps),
    )(*operands)


def per_device(order, patches, ln_gain, w_qkv, qk_gains, w_out):
    rows, width = patches.shape
    count = lax.axis_size("blk")
    place = {index: i for i, index in enumerate(order)}

    def onward(right_core):
        return [
            (h * count + b, (1 - h) * count + order[(place[b] + step) % count])
            for b in range(count)
            for h, step in ((right_core, 1), (1 - right_core, -1))
        ]

    hops = (onward(0), onward(1))
    axes = ("head", "blk")
    swap = [(0, 1), (1, 0)]

    shape = jax.ShapeDtypeStruct
    tie = lax.optimization_barrier
    (ones,) = call(same_head_kernel, [shape((SPAN, SPAN), BF16)], (), 10_000_000_000)
    one = lax.ppermute(patches, axes, hops[0])
    sibling = lax.ppermute(patches, "head", swap)
    gain = ln_gain.reshape(1, width)
    gain, ones = tie((gain, ones))
    normed, other = call(
        normalise_kernel,
        [shape((rows, width), BF16)] * 2,
        (patches, sibling, gain, w_qkv),
        0,
    )
    two = lax.ppermute(normed, axes, hops[1])
    (query,) = call(
        query_kernel,
        [shape((width, 2 * rows), BF16)],
        (normed, other, w_qkv, qk_gains, ones),
        2 * 2 * rows * width * width,
    )
    state_shapes = [
        shape((H, 2 * rows), F32),
        shape((H, 2 * rows), F32),
        shape((width, 2 * rows), F32),
    ]
    last_shapes = [
        shape((width, rows), F32),
        shape((width, rows), BF16),
        shape((2 * H, rows), F32),
        shape((2 * H, rows), F32),
    ]
    flops = 2 * rows * width * 2 * width + 2 * 2 * rows * 2 * rows * width

    def take(blocks, state, last=False):
        arrays, raws = zip(*blocks)
        return call(
            functools.partial(absorb, not state, last, raws),
            last_shapes if last else state_shapes,
            (*arrays, w_qkv, gain, qk_gains, ones, query, *state),
            len(blocks) * flops,
            len(blocks) * H * rows * 2 * rows,
        )

    one, query = tie((one, query))
    late, state = (normed, False), ()
    for turn in range(1, count // 2):
        here_one, here_two = one, two
        one = lax.ppermute(here_one, axes, hops[turn % 2])
        if turn < count // 2 - 1:
            state, here_two = tie((take([late], state), here_two))
            two = lax.ppermute(here_two, axes, hops[(turn + 1) % 2])
            state, one = tie((take([(here_one, True)], state), one))
            late = here_two, False
    state, here_two = tie((take([late, (here_one, True)], state), here_two))
    state, one = tie((take([(here_two, False)], state), one))
    mine, theirs, my_state, their_state = take([(one, True)], state, last=True)
    theirs = lax.ppermute(theirs, "head", swap)
    their_state = lax.ppermute(their_state, "head", swap)
    return call(
        finish_kernel,
        [shape((rows, width), BF16)],
        (mine, theirs, my_state, their_state, w_out),
        2 * rows * width * width,
    )[0]


def solution(mesh):
    placed = (P(("group", "head", "blk"), None), P(), P(), P(), P())
    return jax.shard_map(
        functools.partial(per_device, ring_order(mesh)),
        mesh=mesh,
        in_specs=placed,
        out_specs=P(("group", "head", "blk"), None),
        check_vma=False,
    )
```

```python
import functools
import math

import jax
import jax.numpy as jnp
from jax import lax
from jax.experimental import pallas as pl
from jax.experimental.pallas import tpu as pltpu
from jax.sharding import PartitionSpec as P

H = 16
HD = 64
PAIR = 2 * HD
SPAN = 4 * HD
SCALE = HD**-0.5 * math.log2(math.e)
F32 = jnp.float32
BF16 = jnp.bfloat16
VMEM = pl.BlockSpec(memory_space=pltpu.VMEM)


def ring_order(mesh):
    axis = mesh.axis_names.index("blk")
    along = mesh.devices
    for other in reversed(range(along.ndim)):
        if other != axis:
            along = along.take(0, axis=other)
    count = along.shape[0]
    coords = [getattr(device, "coords", None) for device in along]
    if any(c is None for c in coords):
        return list(range(count))
    place = {tuple(c): i for i, c in enumerate(coords)}
    varying = [a for a in range(3) if len({c[a] for c in place}) > 1]
    if len(place) != count or len(varying) != 2:
        return list(range(count))
    short, long = sorted(varying, key=lambda a: len({c[a] for c in place}))
    columns = sorted({c[short] for c in place})
    if len(columns) != 2:
        return list(range(count))
    up = sorted((c for c in place if c[short] == columns[0]), key=lambda c: c[long])
    down = sorted((c for c in place if c[short] == columns[1]), key=lambda c: -c[long])
    return [place[c] for c in up + down]


def same_head_kernel(out_ref):
    row = lax.broadcasted_iota(jnp.int32, out_ref.shape, 0) // HD
    column = lax.broadcasted_iota(jnp.int32, out_ref.shape, 1) // HD
    out_ref[...] = jnp.where(row == column, 1.0, 0.0).astype(BF16)


def normalised(block, gain):
    values = block.astype(F32)
    centre = values - jnp.mean(values, axis=-1, keepdims=True)
    variance = jnp.mean(centre * centre, axis=-1, keepdims=True)
    return (centre * lax.rsqrt(variance + 1e-05) * gain).astype(BF16)


def head_norm(columns, gain, ones):
    squares = jnp.dot((columns * columns).astype(BF16), ones, preferred_element_type=F32)
    return (columns * lax.rsqrt(squares * (1.0 / HD) + 1e-06) * gain).astype(BF16)


def normalise_kernel(own_ref, sibling_ref, gain_ref, w_ref, out_ref, other_ref):
    for ref, block_ref in ((out_ref, own_ref), (other_ref, sibling_ref)):
        ref[...] = normalised(block_ref[...], gain_ref[...])


def query_kernel(own_ref, sibling_ref, w_ref, gains_ref, ones_ref, query_ref):
    rows, width = own_ref.shape
    ones = ones_ref[...]
    spans = [slice(at, at + SPAN) for at in range(0, width, SPAN)]
    projected = [
        (i, span, jnp.dot(ref[...], w_ref[:, span], preferred_element_type=F32))
        for i, ref in enumerate((own_ref, sibling_ref))
        for span in spans
    ]
    for i, span, columns in projected:
        query = head_norm(columns, gains_ref[0:1, span] * SCALE, ones)
        query_ref[span, i * rows : (i + 1) * rows] = query.astype(F32).T.astype(BF16)


def absorb(first, last, raws, *refs):
    blocks, refs = refs[: len(raws)], refs[len(raws) :]
    w_ref, gain_ref, gains_ref, ones_ref, q_ref = refs[:5]
    if first:
        outs = refs[5:]
    else:
        (max_ref, sum_ref, acc_ref), outs = refs[5:8], refs[8:]
        old_max, old_sum = max_ref[...], sum_ref[...]
    width, queries = q_ref.shape
    half = queries // 2
    heads = SPAN // HD
    blocks = [
        normalised(ref[...], gain_ref[...]) if raw else ref[...] for ref, raw in zip(blocks, raws)
    ]
    block = jnp.concatenate(blocks, axis=0) if len(blocks) > 1 else blocks[0]
    ones = ones_ref[...]
    zeros = jnp.zeros((HD, queries), BF16)
    counts = jnp.ones((16, block.shape[0]), BF16)
    held = {}
    maxima, sums = [], []

    def project(i):
        for name, at in (("key", width), ("value", 2 * width)):
            span = slice(at + i * SPAN, at + (i + 1) * SPAN)
            held[name, i] = jnp.dot(block, w_ref[:, span], preferred_element_type=F32)

    def norm(i):
        span = slice(i * SPAN, (i + 1) * SPAN)
        held["key", i] = head_norm(held["key", i], gains_ref[1:2, span], ones)
        held["value", i] = held["value", i].T.astype(BF16)

    def score(i):
        keys = held.pop(("key", i))
        for j in range(heads):
            at = i * SPAN + j * HD
            pair = j // 2 * PAIR
            query = q_ref[at : at + HD, :]
            query = jnp.concatenate([query, zeros] if j % 2 == 0 else [zeros, query], axis=0)
            held["score", i, j] = jnp.dot(
                keys[:, pair : pair + PAIR], query, preferred_element_type=F32
            )

    def soften(i):
        scores = [held.pop(("score", i, j)) for j in range(heads)]
        top = jnp.concatenate([jnp.max(s, axis=0, keepdims=True) for s in scores], axis=0)
        if not first:
            before = old_max[i * heads : (i + 1) * heads]
            top = jnp.maximum(top, before)
            held["shrink", i] = jnp.exp2(before - top)
        exponents = [jnp.exp2(s - top[j : j + 1]) for j, s in enumerate(scores)]
        maxima.append(top)
        for j, exponent in enumerate(exponents):
            held["weight", i, j] = exponent.astype(BF16)

    def weigh(i):
        values = held.pop(("value", i))
        for j in range(heads):
            at = i * SPAN + j * HD
            added = jnp.dot(
                jnp.concatenate([values[j * HD : (j + 1) * HD], counts], axis=0),
                held.pop(("weight", i, j)),
                preferred_element_type=F32,
            )
            total, added = added[HD : HD + 1], added[:HD]
            if not first:
                shrink = held["shrink", i][j : j + 1]
                total = total + old_sum[i * heads + j : i * heads + j + 1] * shrink
                added = added + acc_ref[at : at + HD, :] * shrink
            sums.append(total)
            if last:
                for ref, part in zip(outs[:2], halves):
                    ref[at : at + HD, :] = added[:, part].astype(ref.dtype)
            else:
                outs[2][at : at + HD, :] = added

    halves = (slice(0, half), slice(half, queries))
    stages = (project, norm, score, soften, weigh)
    for turn in range(width // SPAN + len(stages) - 1):
        for behind, stage in enumerate(stages):
            if 0 <= turn - behind < width // SPAN:
                stage(turn - behind)
    top, total = jnp.concatenate(maxima, axis=0), jnp.concatenate(sums, axis=0)
    if last:
        for ref, part in zip(outs[2:], halves):
            ref[:H, :] = top[:, part]
            ref[H:, :] = total[:, part]
    else:
        outs[0][...] = top
        outs[1][...] = total


def finish_kernel(mine_ref, theirs_ref, my_state_ref, their_state_ref, w_ref, out_ref):
    width = mine_ref.shape[0]
    top = jnp.maximum(my_state_ref[:H, :], their_state_ref[:H, :])
    mine = jnp.exp2(my_state_ref[:H, :] - top)
    theirs = jnp.exp2(their_state_ref[:H, :] - top)
    total = my_state_ref[H:, :] * mine + their_state_ref[H:, :] * theirs
    mine, theirs = mine / total, theirs / total
    spans = []
    for at in range(0, width, SPAN):
        merged = [
            mine_ref[h * HD : (h + 1) * HD, :] * mine[h : h + 1]
            + theirs_ref[h * HD : (h + 1) * HD, :].astype(F32) * theirs[h : h + 1]
            for h in range(at // HD, (at + SPAN) // HD)
        ]
        spans.append(jnp.concatenate(merged, axis=0).T.astype(BF16))
    attended = jnp.concatenate(spans, axis=1)
    out_ref[...] = jnp.dot(attended, w_ref[...], preferred_element_type=F32).astype(BF16)


def call(body, outs, operands, flops, exps=0):
    moved = sum(a.size * a.dtype.itemsize for a in (*operands, *outs))
    return pl.pallas_call(
        body,
        out_shape=outs,
        in_specs=[VMEM] * len(operands),
        out_specs=[VMEM] * len(outs),
        compiler_params=pltpu.CompilerParams(vmem_limit_bytes=24 * 1024 * 1024),
        cost_estimate=pl.CostEstimate(flops=flops, bytes_accessed=moved, transcendentals=exps),
    )(*operands)


def per_device(order, patches, ln_gain, w_qkv, qk_gains, w_out):
    rows, width = patches.shape
    count = lax.axis_size("blk")
    place = {index: i for i, index in enumerate(order)}

    def onward(right_core):
        return [
            (h * count + b, (1 - h) * count + order[(place[b] + step) % count])
            for b in range(count)
            for h, step in ((right_core, 1), (1 - right_core, -1))
        ]

    hops = (onward(1), onward(0))
    axes = ("head", "blk")
    swap = [(0, 1), (1, 0)]

    shape = jax.ShapeDtypeStruct
    tie = lax.optimization_barrier
    (ones,) = call(same_head_kernel, [shape((SPAN, SPAN), BF16)], (), 10_000_000_000)
    one = lax.ppermute(patches, axes, hops[0])
    sibling = lax.ppermute(patches, "head", swap)
    gain = ln_gain.reshape(1, width)
    gain, ones = tie((gain, ones))
    normed, other = call(
        normalise_kernel,
        [shape((rows, width), BF16)] * 2,
        (patches, sibling, gain, w_qkv),
        0,
    )
    two = lax.ppermute(other, axes, hops[0])
    (query,) = call(
        query_kernel,
        [shape((width, 2 * rows), BF16)],
        (normed, other, w_qkv, qk_gains, ones),
        2 * 2 * rows * width * width,
    )
    state_shapes = [
        shape((H, 2 * rows), F32),
        shape((H, 2 * rows), F32),
        shape((width, 2 * rows), F32),
    ]
    last_shapes = [
        shape((width, rows), F32),
        shape((width, rows), BF16),
        shape((2 * H, rows), F32),
        shape((2 * H, rows), F32),
    ]
    flops = 2 * rows * width * 2 * width + 2 * 2 * rows * 2 * rows * width

    def take(blocks, state, last=False):
        arrays, raws = zip(*blocks)
        return call(
            functools.partial(absorb, not state, last, raws),
            last_shapes if last else state_shapes,
            (*arrays, w_qkv, gain, qk_gains, ones, query, *state),
            len(blocks) * flops,
            len(blocks) * H * rows * 2 * rows,
        )

    one, query = tie((one, query))
    late, state = (normed, False), ()
    for turn in range(1, count // 2):
        here_one, here_two = one, two
        one = lax.ppermute(here_one, axes, hops[turn % 2])
        if turn < count // 2 - 1:
            state, here_two = tie((take([late], state), here_two))
            two = lax.ppermute(here_two, axes, hops[turn % 2])
            state, one = tie((take([(here_one, True)], state), one))
            late = here_two, False
    state, here_two = tie((take([late, (here_one, True)], state), here_two))
    state, one = tie((take([(here_two, False)], state), one))
    mine, theirs, my_state, their_state = take([(one, True)], state, last=True)
    theirs = lax.ppermute(theirs, "head", swap)
    their_state = lax.ppermute(their_state, "head", swap)
    return call(
        finish_kernel,
        [shape((rows, width), BF16)],
        (mine, theirs, my_state, their_state, w_out),
        2 * rows * width * width,
    )[0]


def solution(mesh):
    placed = (P(("group", "head", "blk"), None), P(), P(), P(), P())
    return jax.shard_map(
        functools.partial(per_device, ring_order(mesh)),
        mesh=mesh,
        in_specs=placed,
        out_specs=P(("group", "head", "blk"), None),
        check_vma=False,
    )
```

```python
import functools
import math

import jax
import jax.numpy as jnp
from jax import lax
from jax.experimental import pallas as pl
from jax.experimental.pallas import tpu as pltpu
from jax.sharding import PartitionSpec as P

H = 16
HD = 64
PAIR = 2 * HD
SPAN = 4 * HD
SCALE = HD**-0.5 * math.log2(math.e)
F32 = jnp.float32
BF16 = jnp.bfloat16
VMEM = pl.BlockSpec(memory_space=pltpu.VMEM)


def ring_order(mesh):
    axis = mesh.axis_names.index("blk")
    along = mesh.devices
    for other in reversed(range(along.ndim)):
        if other != axis:
            along = along.take(0, axis=other)
    count = along.shape[0]
    coords = [getattr(device, "coords", None) for device in along]
    if any(c is None for c in coords):
        return list(range(count))
    place = {tuple(c): i for i, c in enumerate(coords)}
    varying = [a for a in range(3) if len({c[a] for c in place}) > 1]
    if len(place) != count or len(varying) != 2:
        return list(range(count))
    short, long = sorted(varying, key=lambda a: len({c[a] for c in place}))
    columns = sorted({c[short] for c in place})
    if len(columns) != 2:
        return list(range(count))
    up = sorted((c for c in place if c[short] == columns[0]), key=lambda c: c[long])
    down = sorted((c for c in place if c[short] == columns[1]), key=lambda c: -c[long])
    return [place[c] for c in up + down]


def same_head_kernel(out_ref):
    row = lax.broadcasted_iota(jnp.int32, out_ref.shape, 0) // HD
    column = lax.broadcasted_iota(jnp.int32, out_ref.shape, 1) // HD
    out_ref[...] = jnp.where(row == column, 1.0, 0.0).astype(BF16)


def normalised(block, gain):
    values = block.astype(F32)
    centre = values - jnp.mean(values, axis=-1, keepdims=True)
    variance = jnp.mean(centre * centre, axis=-1, keepdims=True)
    return (centre * lax.rsqrt(variance + 1e-05) * gain).astype(BF16)


def head_norm(columns, gain, ones):
    squares = jnp.dot((columns * columns).astype(BF16), ones, preferred_element_type=F32)
    return (columns * lax.rsqrt(squares * (1.0 / HD) + 1e-06) * gain).astype(BF16)


def normalise_kernel(own_ref, sibling_ref, gain_ref, w_ref, out_ref, other_ref):
    for ref, block_ref in ((out_ref, own_ref), (other_ref, sibling_ref)):
        ref[...] = normalised(block_ref[...], gain_ref[...])


def query_kernel(own_ref, sibling_ref, w_ref, gains_ref, ones_ref, query_ref):
    rows, width = own_ref.shape
    ones = ones_ref[...]
    spans = [slice(at, at + SPAN) for at in range(0, width, SPAN)]
    projected = [
        (i, span, jnp.dot(ref[...], w_ref[:, span], preferred_element_type=F32))
        for i, ref in enumerate((own_ref, sibling_ref))
        for span in spans
    ]
    for i, span, columns in projected:
        query = head_norm(columns, gains_ref[0:1, span] * SCALE, ones)
        query_ref[span, i * rows : (i + 1) * rows] = query.astype(F32).T.astype(BF16)


def pipeline(stages, count):
    for turn in range(count + len(stages) - 1):
        for behind, stage in enumerate(stages):
            if 0 <= turn - behind < count:
                stage(turn - behind)


def absorb(first, raws, *refs):
    blocks, refs = refs[: len(raws)], refs[len(raws) :]
    w_ref, gain_ref, gains_ref, ones_ref, q_ref = refs[:5]
    if first:
        outs = refs[5:]
    else:
        (max_ref, sum_ref, acc_ref), outs = refs[5:8], refs[8:]
        old_max, old_sum = max_ref[...], sum_ref[...]
    width, queries = q_ref.shape
    heads = SPAN // HD
    blocks = [
        normalised(ref[...], gain_ref[...]) if raw else ref[...] for ref, raw in zip(blocks, raws)
    ]
    block = jnp.concatenate(blocks, axis=0) if len(blocks) > 1 else blocks[0]
    ones = ones_ref[...]
    zeros = jnp.zeros((HD, queries), BF16)
    counts = jnp.ones((16, block.shape[0]), BF16)
    held = {}
    maxima, sums = [], []

    def project(i):
        for name, at in (("key", width), ("value", 2 * width)):
            span = slice(at + i * SPAN, at + (i + 1) * SPAN)
            held[name, i] = jnp.dot(block, w_ref[:, span], preferred_element_type=F32)

    def norm(i):
        span = slice(i * SPAN, (i + 1) * SPAN)
        held["key", i] = head_norm(held["key", i], gains_ref[1:2, span], ones)
        held["value", i] = held["value", i].T.astype(BF16)

    def score(i):
        keys = held.pop(("key", i))
        for j in range(heads):
            at = i * SPAN + j * HD
            pair = j // 2 * PAIR
            query = q_ref[at : at + HD, :]
            query = jnp.concatenate([query, zeros] if j % 2 == 0 else [zeros, query], axis=0)
            held["score", i, j] = jnp.dot(
                keys[:, pair : pair + PAIR], query, preferred_element_type=F32
            )

    def soften(i):
        scores = [held.pop(("score", i, j)) for j in range(heads)]
        top = jnp.concatenate([jnp.max(s, axis=0, keepdims=True) for s in scores], axis=0)
        if not first:
            before = old_max[i * heads : (i + 1) * heads]
            top = jnp.maximum(top, before)
            held["shrink", i] = jnp.exp2(before - top)
        exponents = [jnp.exp2(s - top[j : j + 1]) for j, s in enumerate(scores)]
        maxima.append(top)
        for j, exponent in enumerate(exponents):
            held["weight", i, j] = exponent.astype(BF16)

    def weigh(i):
        values = held.pop(("value", i))
        for j in range(heads):
            at = i * SPAN + j * HD
            added = jnp.dot(
                jnp.concatenate([values[j * HD : (j + 1) * HD], counts], axis=0),
                held.pop(("weight", i, j)),
                preferred_element_type=F32,
            )
            total, added = added[HD : HD + 1], added[:HD]
            if not first:
                shrink = held["shrink", i][j : j + 1]
                total = total + old_sum[i * heads + j : i * heads + j + 1] * shrink
                added = added + acc_ref[at : at + HD, :] * shrink
            sums.append(total)
            outs[2][at : at + HD, :] = added

    pipeline((project, norm, score, soften, weigh), width // SPAN)
    top, total = jnp.concatenate(maxima, axis=0), jnp.concatenate(sums, axis=0)
    outs[0][...] = top
    outs[1][...] = total


def half_stages(held, part, q_ref, max_ref, sum_ref, acc_ref, put):
    old_max, old_sum = max_ref[:, part], sum_ref[:, part]
    half = old_max.shape[1]
    zeros = jnp.zeros((HD, half), BF16)
    pairs = [(j, slice(j * PAIR, (j + 1) * PAIR)) for j in range(SPAN // PAIR)]
    maxima, sums = [], []

    def beside(rows, i, j):
        head = (i * SPAN + j * PAIR) // HD
        return jnp.concatenate([rows[head : head + 1], rows[head + 1 : head + 2]], axis=1)

    def score(i):
        keys = held.pop(("key", i))
        for j, pair in pairs:
            at = i * SPAN + j * PAIR
            even, odd = q_ref[at : at + HD, part], q_ref[at + HD : at + PAIR, part]
            query = jnp.concatenate(
                [jnp.concatenate([even, zeros], axis=1), jnp.concatenate([zeros, odd], axis=1)],
                axis=0,
            )
            held["score", i, j] = jnp.dot(keys[:, pair], query, preferred_element_type=F32)

    def soften(i):
        for j, _ in pairs:
            scores, before = held.pop(("score", i, j)), beside(old_max, i, j)
            top = jnp.maximum(jnp.max(scores, axis=0, keepdims=True), before)
            held["shrink", i, j] = jnp.exp2(before - top)
            held["weight", i, j] = jnp.exp2(scores - top).astype(BF16)
            maxima.extend([top[:, :half], top[:, half:]])

    def weigh(i):
        values = held.pop(("value", i))
        counts = jnp.ones((16, values.shape[1]), BF16)
        for j, pair in pairs:
            both = jnp.dot(
                jnp.concatenate([values[pair], counts], axis=0),
                held.pop(("weight", i, j)),
                preferred_element_type=F32,
            )
            shrink = held.pop(("shrink", i, j))
            total = both[PAIR : PAIR + 1] + beside(old_sum, i, j) * shrink
            sums.extend([total[:, :half], total[:, half:]])
            for k, side in enumerate((slice(0, half), slice(half, 2 * half))):
                at = i * SPAN + j * PAIR + k * HD
                added = both[k * HD : (k + 1) * HD, side]
                put(at, added + acc_ref[at : at + HD, part] * shrink[:, side])

    return (score, soften, weigh), maxima, sums


def send_kernel(
    block_ref, w_ref, gain_ref, gains_ref, ones_ref, q_ref, max_ref, sum_ref, acc_ref,
    sent_ref, sent_state_ref, keys_ref, values_ref,
):
    width, queries = q_ref.shape
    block = normalised(block_ref[...], gain_ref[...])
    ones = ones_ref[...]
    held = {}

    def project(i):
        for name, at in (("key", width), ("value", 2 * width)):
            span = slice(at + i * SPAN, at + (i + 1) * SPAN)
            held[name, i] = jnp.dot(block, w_ref[:, span], preferred_element_type=F32)

    def norm(i):
        span = slice(i * SPAN, (i + 1) * SPAN)
        keys_ref[:, span] = held["key", i] = head_norm(held["key", i], gains_ref[1:2, span], ones)
        values_ref[span, :] = held["value", i] = held["value", i].T.astype(BF16)

    def put(at, rows):
        sent_ref[at : at + HD, :] = rows.astype(BF16)

    part = slice(queries // 2, queries)
    stages, maxima, sums = half_stages(held, part, q_ref, max_ref, sum_ref, acc_ref, put)
    pipeline((project, norm, *stages), width // SPAN)
    top, total = jnp.concatenate(maxima, axis=0), jnp.concatenate(sums, axis=0)
    sent_state_ref[:H, :] = top
    sent_state_ref[H:, :] = total


def keep_kernel(
    keys_ref, values_ref, q_ref, max_ref, sum_ref, acc_ref, mine_ref, state_ref
):
    width, queries = q_ref.shape
    held = {}
    for i in range(width // SPAN):
        span = slice(i * SPAN, (i + 1) * SPAN)
        held["key", i], held["value", i] = keys_ref[:, span], values_ref[span, :]

    def put(at, rows):
        mine_ref[at : at + HD, :] = rows

    part = slice(0, queries // 2)
    stages, maxima, sums = half_stages(held, part, q_ref, max_ref, sum_ref, acc_ref, put)
    pipeline(stages, width // SPAN)
    state_ref[:H, :] = jnp.concatenate(maxima, axis=0)
    state_ref[H:, :] = jnp.concatenate(sums, axis=0)


def finish_kernel(mine_ref, theirs_ref, my_state_ref, their_state_ref, w_ref, out_ref):
    width = mine_ref.shape[0]
    top = jnp.maximum(my_state_ref[:H, :], their_state_ref[:H, :])
    mine = jnp.exp2(my_state_ref[:H, :] - top)
    theirs = jnp.exp2(their_state_ref[:H, :] - top)
    total = my_state_ref[H:, :] * mine + their_state_ref[H:, :] * theirs
    mine, theirs = mine / total, theirs / total
    spans = []
    for at in range(0, width, SPAN):
        merged = [
            mine_ref[h * HD : (h + 1) * HD, :] * mine[h : h + 1]
            + theirs_ref[h * HD : (h + 1) * HD, :].astype(F32) * theirs[h : h + 1]
            for h in range(at // HD, (at + SPAN) // HD)
        ]
        spans.append(jnp.concatenate(merged, axis=0).T.astype(BF16))
    attended = jnp.concatenate(spans, axis=1)
    out_ref[...] = jnp.dot(attended, w_ref[...], preferred_element_type=F32).astype(BF16)


def call(body, outs, operands, flops, exps=0):
    moved = sum(a.size * a.dtype.itemsize for a in (*operands, *outs))
    return pl.pallas_call(
        body,
        out_shape=outs,
        in_specs=[VMEM] * len(operands),
        out_specs=[VMEM] * len(outs),
        compiler_params=pltpu.CompilerParams(vmem_limit_bytes=24 * 1024 * 1024),
        cost_estimate=pl.CostEstimate(flops=flops, bytes_accessed=moved, transcendentals=exps),
    )(*operands)


def per_device(order, patches, ln_gain, w_qkv, qk_gains, w_out):
    rows, width = patches.shape
    count = lax.axis_size("blk")
    place = {index: i for i, index in enumerate(order)}

    def onward(right_core):
        return [
            (h * count + b, (1 - h) * count + order[(place[b] + step) % count])
            for b in range(count)
            for h, step in ((right_core, 1), (1 - right_core, -1))
        ]

    hops = (onward(1), onward(0))
    axes = ("head", "blk")
    swap = [(0, 1), (1, 0)]

    shape = jax.ShapeDtypeStruct
    tie = lax.optimization_barrier
    (ones,) = call(same_head_kernel, [shape((SPAN, SPAN), BF16)], (), 10_000_000_000)
    one = lax.ppermute(patches, axes, hops[0])
    sibling = lax.ppermute(patches, "head", swap)
    gain = ln_gain.reshape(1, width)
    gain, ones = tie((gain, ones))
    normed, other = call(
        normalise_kernel,
        [shape((rows, width), BF16)] * 2,
        (patches, sibling, gain, w_qkv),
        0,
    )
    two = lax.ppermute(other, axes, hops[0])
    (query,) = call(
        query_kernel,
        [shape((width, 2 * rows), BF16)],
        (normed, other, w_qkv, qk_gains, ones),
        2 * 2 * rows * width * width,
    )
    state_shapes = [
        shape((H, 2 * rows), F32),
        shape((H, 2 * rows), F32),
        shape((width, 2 * rows), F32),
    ]
    flops = 2 * rows * width * 2 * width + 2 * 2 * rows * 2 * rows * width

    def take(blocks, state):
        arrays, raws = zip(*blocks)
        return call(
            functools.partial(absorb, not state, raws),
            state_shapes,
            (*arrays, w_qkv, gain, qk_gains, ones, query, *state),
            len(blocks) * flops,
            len(blocks) * H * rows * 2 * rows,
        )

    one, query = tie((one, query))
    late, state = (normed, False), ()
    for turn in range(1, count // 2):
        here_one, here_two = one, two
        one = lax.ppermute(here_one, axes, hops[turn % 2])
        if turn < count // 2 - 1:
            state, here_two = tie((take([late], state), here_two))
            two = lax.ppermute(here_two, axes, hops[turn % 2])
            state, one = tie((take([(here_one, True)], state), one))
            late = here_two, False
    state, here_two = tie((take([late, (here_one, True)], state), here_two))
    state, one = tie((take([(here_two, False)], state), one))
    sent, sent_state, keys, values = call(
        send_kernel,
        [
            shape((width, rows), BF16),
            shape((2 * H, rows), F32),
            shape((rows, width), BF16),
            shape((width, rows), BF16),
        ],
        (one, w_qkv, gain, qk_gains, ones, query, *state),
        flops,
        H * rows * rows,
    )
    theirs = lax.ppermute(sent, "head", swap)
    their_state = lax.ppermute(sent_state, "head", swap)
    mine, my_state = call(
        keep_kernel,
        [shape((width, rows), F32), shape((2 * H, rows), F32)],
        (keys, values, query, *state),
        flops // 4,
        H * rows * rows,
    )
    return call(
        finish_kernel,
        [shape((rows, width), BF16)],
        (mine, theirs, my_state, their_state, w_out),
        2 * rows * width * width,
    )[0]


def solution(mesh):
    placed = (P(("group", "head", "blk"), None), P(), P(), P(), P())
    return jax.shard_map(
        functools.partial(per_device, ring_order(mesh)),
        mesh=mesh,
        in_specs=placed,
        out_specs=P(("group", "head", "blk"), None),
        check_vma=False,
    )
```

```python
import functools
import math

import jax
import jax.numpy as jnp
from jax import lax
from jax.experimental import pallas as pl
from jax.experimental.pallas import tpu as pltpu
from jax.sharding import PartitionSpec as P

H = 16
HD = 64
PAIR = 2 * HD
SPAN = 4 * HD
SCALE = HD**-0.5 * math.log2(math.e)
F32 = jnp.float32
BF16 = jnp.bfloat16
VMEM = pl.BlockSpec(memory_space=pltpu.VMEM)


def ring_order(mesh):
    axis = mesh.axis_names.index("blk")
    along = mesh.devices
    for other in reversed(range(along.ndim)):
        if other != axis:
            along = along.take(0, axis=other)
    count = along.shape[0]
    coords = [getattr(device, "coords", None) for device in along]
    if any(c is None for c in coords):
        return list(range(count))
    place = {tuple(c): i for i, c in enumerate(coords)}
    varying = [a for a in range(3) if len({c[a] for c in place}) > 1]
    if len(place) != count or len(varying) != 2:
        return list(range(count))
    short, long = sorted(varying, key=lambda a: len({c[a] for c in place}))
    columns = sorted({c[short] for c in place})
    if len(columns) != 2:
        return list(range(count))
    up = sorted((c for c in place if c[short] == columns[0]), key=lambda c: c[long])
    down = sorted((c for c in place if c[short] == columns[1]), key=lambda c: -c[long])
    return [place[c] for c in up + down]


def same_head_kernel(out_ref):
    row = lax.broadcasted_iota(jnp.int32, out_ref.shape, 0) // HD
    column = lax.broadcasted_iota(jnp.int32, out_ref.shape, 1) // HD
    out_ref[...] = jnp.where(row == column, 1.0, 0.0).astype(BF16)


def normalised(block, gain):
    values = block.astype(F32)
    centre = values - jnp.mean(values, axis=-1, keepdims=True)
    variance = jnp.mean(centre * centre, axis=-1, keepdims=True)
    return (centre * lax.rsqrt(variance + 1e-05) * gain).astype(BF16)


def head_norm(columns, gain, ones):
    squares = jnp.dot((columns * columns).astype(BF16), ones, preferred_element_type=F32)
    return (columns * lax.rsqrt(squares * (1.0 / HD) + 1e-06) * gain).astype(BF16)


def normalise_kernel(own_ref, sibling_ref, gain_ref, w_ref, out_ref, other_ref):
    for ref, block_ref in ((out_ref, own_ref), (other_ref, sibling_ref)):
        ref[...] = normalised(block_ref[...], gain_ref[...])


def query_kernel(own_ref, sibling_ref, w_ref, gains_ref, ones_ref, query_ref):
    rows, width = own_ref.shape
    ones = ones_ref[...]
    spans = [slice(at, at + SPAN) for at in range(0, width, SPAN)]
    projected = [
        (i, span, jnp.dot(ref[...], w_ref[:, span], preferred_element_type=F32))
        for i, ref in enumerate((own_ref, sibling_ref))
        for span in spans
    ]
    for i, span, columns in projected:
        query = head_norm(columns, gains_ref[0:1, span] * SCALE, ones)
        query_ref[span, i * rows : (i + 1) * rows] = query.astype(F32).T.astype(BF16)


def pipeline(stages, count):
    for turn in range(count + len(stages) - 1):
        for behind, stage in enumerate(stages):
            if 0 <= turn - behind < count:
                stage(turn - behind)


def absorb(first, raws, *refs):
    blocks, refs = refs[: len(raws)], refs[len(raws) :]
    w_ref, gain_ref, gains_ref, ones_ref, q_ref = refs[:5]
    if first:
        outs = refs[5:]
    else:
        (max_ref, sum_ref, acc_ref), outs = refs[5:8], refs[8:]
        old_max, old_sum = max_ref[...], sum_ref[...]
    width, queries = q_ref.shape
    heads = SPAN // HD
    blocks = [
        normalised(ref[...], gain_ref[...]) if raw else ref[...] for ref, raw in zip(blocks, raws)
    ]
    block = jnp.concatenate(blocks, axis=0) if len(blocks) > 1 else blocks[0]
    ones = ones_ref[...]
    zeros = jnp.zeros((HD, queries), BF16)
    counts = jnp.ones((16, block.shape[0]), BF16)
    held = {}
    maxima, sums = [], []

    def project(i):
        for name, at in (("key", width), ("value", 2 * width)):
            span = slice(at + i * SPAN, at + (i + 1) * SPAN)
            held[name, i] = jnp.dot(block, w_ref[:, span], preferred_element_type=F32)

    def norm(i):
        span = slice(i * SPAN, (i + 1) * SPAN)
        held["key", i] = head_norm(held["key", i], gains_ref[1:2, span], ones)
        held["value", i] = held["value", i].T.astype(BF16)

    def score(i):
        keys = held.pop(("key", i))
        for j in range(heads):
            at = i * SPAN + j * HD
            pair = j // 2 * PAIR
            query = q_ref[at : at + HD, :]
            query = jnp.concatenate([query, zeros] if j % 2 == 0 else [zeros, query], axis=0)
            held["score", i, j] = jnp.dot(
                keys[:, pair : pair + PAIR], query, preferred_element_type=F32
            )

    def soften(i):
        scores = [held.pop(("score", i, j)) for j in range(heads)]
        top = jnp.concatenate([jnp.max(s, axis=0, keepdims=True) for s in scores], axis=0)
        if not first:
            before = old_max[i * heads : (i + 1) * heads]
            top = jnp.maximum(top, before)
            held["shrink", i] = jnp.exp2(before - top)
        exponents = [jnp.exp2(s - top[j : j + 1]) for j, s in enumerate(scores)]
        maxima.append(top)
        for j, exponent in enumerate(exponents):
            held["weight", i, j] = exponent.astype(BF16)

    def weigh(i):
        values = held.pop(("value", i))
        for j in range(heads):
            at = i * SPAN + j * HD
            added = jnp.dot(
                jnp.concatenate([values[j * HD : (j + 1) * HD], counts], axis=0),
                held.pop(("weight", i, j)),
                preferred_element_type=F32,
            )
            total, added = added[HD : HD + 1], added[:HD]
            if not first:
                shrink = held["shrink", i][j : j + 1]
                total = total + old_sum[i * heads + j : i * heads + j + 1] * shrink
                added = added + acc_ref[at : at + HD, :] * shrink
            sums.append(total)
            outs[2][at : at + HD, :] = added

    pipeline((project, norm, score, soften, weigh), width // SPAN)
    top, total = jnp.concatenate(maxima, axis=0), jnp.concatenate(sums, axis=0)
    outs[0][...] = top
    outs[1][...] = total


def parted(values):
    high = values.astype(BF16)
    rest = values - high.astype(F32)
    middle = rest.astype(BF16)
    return high, middle, (rest - middle.astype(F32)).astype(BF16)


def half_stages(held, part, q_ref, max_ref, sum_ref, acc_ref, put):
    old_max, old_sum = max_ref[:, part], sum_ref[:, part]
    half = old_max.shape[1]
    zeros = jnp.zeros((HD, half), BF16)
    pairs = [(j, slice(j * PAIR, (j + 1) * PAIR)) for j in range(SPAN // PAIR)]
    maxima, sums = [], []

    def beside(rows, i, j):
        head = (i * SPAN + j * PAIR) // HD
        return jnp.concatenate([rows[head : head + 1], rows[head + 1 : head + 2]], axis=1)

    def score(i):
        keys = held.pop(("key", i))
        for j, pair in pairs:
            at = i * SPAN + j * PAIR
            even, odd = q_ref[at : at + HD, part], q_ref[at + HD : at + PAIR, part]
            query = jnp.concatenate(
                [jnp.concatenate([even, zeros], axis=1), jnp.concatenate([zeros, odd], axis=1)],
                axis=0,
            )
            held["score", i, j] = jnp.dot(keys[:, pair], query, preferred_element_type=F32)

    def soften(i):
        for j, _ in pairs:
            scores, before = held.pop(("score", i, j)), beside(old_max, i, j)
            top = jnp.maximum(jnp.max(scores, axis=0, keepdims=True), before)
            held["shrink", i, j] = jnp.exp2(before - top)
            held["weight", i, j] = jnp.exp2(scores - top).astype(BF16)
            maxima.extend([top[:, :half], top[:, half:]])

    def weigh(i):
        values = held.pop(("value", i))
        counts = jnp.ones((16, values.shape[1]), BF16)
        for j, pair in pairs:
            both = jnp.dot(
                jnp.concatenate([values[pair], counts], axis=0),
                held.pop(("weight", i, j)),
                preferred_element_type=F32,
            )
            shrink = held.pop(("shrink", i, j))
            total = both[PAIR : PAIR + 1] + beside(old_sum, i, j) * shrink
            sums.extend([total[:, :half], total[:, half:]])
            for k, side in enumerate((slice(0, half), slice(half, 2 * half))):
                at = i * SPAN + j * PAIR + k * HD
                added = both[k * HD : (k + 1) * HD, side]
                put(at, added + acc_ref[at : at + HD, part] * shrink[:, side])

    return (score, soften, weigh), maxima, sums


def send_kernel(
    block_ref, w_ref, gain_ref, gains_ref, ones_ref, q_ref, max_ref, sum_ref, acc_ref,
    sent_ref, keys_ref, values_ref,
):
    width, queries = q_ref.shape
    block = normalised(block_ref[...], gain_ref[...])
    ones = ones_ref[...]
    held = {}

    def project(i):
        for name, at in (("key", width), ("value", 2 * width)):
            span = slice(at + i * SPAN, at + (i + 1) * SPAN)
            held[name, i] = jnp.dot(block, w_ref[:, span], preferred_element_type=F32)

    def norm(i):
        span = slice(i * SPAN, (i + 1) * SPAN)
        keys_ref[:, span] = held["key", i] = head_norm(held["key", i], gains_ref[1:2, span], ones)
        values_ref[span, :] = held["value", i] = held["value", i].T.astype(BF16)

    def put(at, rows):
        sent_ref[at : at + HD, :] = rows.astype(BF16)

    part = slice(queries // 2, queries)
    stages, maxima, sums = half_stages(held, part, q_ref, max_ref, sum_ref, acc_ref, put)
    pipeline((project, norm, *stages), width // SPAN)
    top, total = jnp.concatenate(maxima, axis=0), jnp.concatenate(sums, axis=0)
    for i, piece in enumerate((*parted(top), *parted(total))):
        sent_ref[width + i * H : width + (i + 1) * H, :] = piece


def keep_kernel(
    keys_ref, values_ref, q_ref, max_ref, sum_ref, acc_ref, mine_ref, state_ref
):
    width, queries = q_ref.shape
    held = {}
    for i in range(width // SPAN):
        span = slice(i * SPAN, (i + 1) * SPAN)
        held["key", i], held["value", i] = keys_ref[:, span], values_ref[span, :]

    def put(at, rows):
        mine_ref[at : at + HD, :] = rows

    part = slice(0, queries // 2)
    stages, maxima, sums = half_stages(held, part, q_ref, max_ref, sum_ref, acc_ref, put)
    pipeline(stages, width // SPAN)
    state_ref[:H, :] = jnp.concatenate(maxima, axis=0)
    state_ref[H:, :] = jnp.concatenate(sums, axis=0)


def finish_kernel(mine_ref, my_state_ref, theirs_ref, w_ref, out_ref):
    width = mine_ref.shape[0]
    pieces = [theirs_ref[at : at + H, :].astype(F32) for at in range(width, theirs_ref.shape[0], H)]
    their_top, their_total = sum(pieces[1:3], pieces[0]), sum(pieces[4:6], pieces[3])
    top = jnp.maximum(my_state_ref[:H, :], their_top)
    mine, theirs = jnp.exp2(my_state_ref[:H, :] - top), jnp.exp2(their_top - top)
    total = my_state_ref[H:, :] * mine + their_total * theirs
    mine, theirs = mine / total, theirs / total
    spans = []
    for at in range(0, width, SPAN):
        merged = [
            mine_ref[h * HD : (h + 1) * HD, :] * mine[h : h + 1]
            + theirs_ref[h * HD : (h + 1) * HD, :].astype(F32) * theirs[h : h + 1]
            for h in range(at // HD, (at + SPAN) // HD)
        ]
        spans.append(jnp.concatenate(merged, axis=0).T.astype(BF16))
    attended = jnp.concatenate(spans, axis=1)
    out_ref[...] = jnp.dot(attended, w_ref[...], preferred_element_type=F32).astype(BF16)


def call(body, outs, operands, flops, exps=0):
    moved = sum(a.size * a.dtype.itemsize for a in (*operands, *outs))
    return pl.pallas_call(
        body,
        out_shape=outs,
        in_specs=[VMEM] * len(operands),
        out_specs=[VMEM] * len(outs),
        compiler_params=pltpu.CompilerParams(vmem_limit_bytes=24 * 1024 * 1024),
        cost_estimate=pl.CostEstimate(flops=flops, bytes_accessed=moved, transcendentals=exps),
    )(*operands)


def per_device(order, patches, ln_gain, w_qkv, qk_gains, w_out):
    rows, width = patches.shape
    count = lax.axis_size("blk")
    place = {index: i for i, index in enumerate(order)}

    def onward(right_core):
        return [
            (h * count + b, (1 - h) * count + order[(place[b] + step) % count])
            for b in range(count)
            for h, step in ((right_core, 1), (1 - right_core, -1))
        ]

    hops = (onward(1), onward(0))
    axes = ("head", "blk")
    swap = [(0, 1), (1, 0)]

    shape = jax.ShapeDtypeStruct
    tie = lax.optimization_barrier
    (ones,) = call(same_head_kernel, [shape((SPAN, SPAN), BF16)], (), 10_000_000_000)
    one = lax.ppermute(patches, axes, hops[0])
    sibling = lax.ppermute(patches, "head", swap)
    gain = ln_gain.reshape(1, width)
    gain, ones = tie((gain, ones))
    normed, other = call(
        normalise_kernel,
        [shape((rows, width), BF16)] * 2,
        (patches, sibling, gain, w_qkv),
        0,
    )
    two = lax.ppermute(other, axes, hops[0])
    (query,) = call(
        query_kernel,
        [shape((width, 2 * rows), BF16)],
        (normed, other, w_qkv, qk_gains, ones),
        2 * 2 * rows * width * width,
    )
    state_shapes = [
        shape((H, 2 * rows), F32),
        shape((H, 2 * rows), F32),
        shape((width, 2 * rows), F32),
    ]
    flops = 2 * rows * width * 2 * width + 2 * 2 * rows * 2 * rows * width

    def take(blocks, state):
        arrays, raws = zip(*blocks)
        return call(
            functools.partial(absorb, not state, raws),
            state_shapes,
            (*arrays, w_qkv, gain, qk_gains, ones, query, *state),
            len(blocks) * flops,
            len(blocks) * H * rows * 2 * rows,
        )

    one, query = tie((one, query))
    late, state = (normed, False), ()
    for turn in range(1, count // 2):
        here_one, here_two = one, two
        one = lax.ppermute(here_one, axes, hops[turn % 2])
        if turn < count // 2 - 1:
            state, here_two = tie((take([late], state), here_two))
            two = lax.ppermute(here_two, axes, hops[turn % 2])
            state, one = tie((take([(here_two, False)], state), one))
            late = here_one, True
    state, here_two = tie((take([late, (here_one, True)], state), here_two))
    state, one = tie((take([(here_two, False)], state), one))
    sent, keys, values = call(
        send_kernel,
        [shape((width + 6 * H, rows), BF16), shape((rows, width), BF16), shape((width, rows), BF16)],
        (one, w_qkv, gain, qk_gains, ones, query, *state),
        flops,
        H * rows * rows,
    )
    came = lax.ppermute(sent, "head", swap)
    mine, my_state = call(
        keep_kernel,
        [shape((width, rows), F32), shape((2 * H, rows), F32)],
        (keys, values, query, *state),
        flops // 4,
        H * rows * rows,
    )
    return call(
        finish_kernel,
        [shape((rows, width), BF16)],
        (mine, my_state, came, w_out),
        2 * rows * width * width,
    )[0]


def solution(mesh):
    placed = (P(("group", "head", "blk"), None), P(), P(), P(), P())
    return jax.shard_map(
        functools.partial(per_device, ring_order(mesh)),
        mesh=mesh,
        in_specs=placed,
        out_specs=P(("group", "head", "blk"), None),
        check_vma=False,
    )
```

```python
import functools
import math

import jax
import jax.numpy as jnp
from jax import lax
from jax.experimental import pallas as pl
from jax.experimental.pallas import tpu as pltpu
from jax.sharding import PartitionSpec as P

H = 16
HD = 64
PAIR = 2 * HD
SPAN = 4 * HD
SCALE = HD**-0.5 * math.log2(math.e)
F32 = jnp.float32
BF16 = jnp.bfloat16
VMEM = pl.BlockSpec(memory_space=pltpu.VMEM)


def ring_order(mesh):
    axis = mesh.axis_names.index("blk")
    along = mesh.devices
    for other in reversed(range(along.ndim)):
        if other != axis:
            along = along.take(0, axis=other)
    count = along.shape[0]
    coords = [getattr(device, "coords", None) for device in along]
    if any(c is None for c in coords):
        return list(range(count))
    place = {tuple(c): i for i, c in enumerate(coords)}
    varying = [a for a in range(3) if len({c[a] for c in place}) > 1]
    if len(place) != count or len(varying) != 2:
        return list(range(count))
    short, long = sorted(varying, key=lambda a: len({c[a] for c in place}))
    columns = sorted({c[short] for c in place})
    if len(columns) != 2:
        return list(range(count))
    up = sorted((c for c in place if c[short] == columns[0]), key=lambda c: c[long])
    down = sorted((c for c in place if c[short] == columns[1]), key=lambda c: -c[long])
    return [place[c] for c in up + down]


def same_head_kernel(out_ref):
    row = lax.broadcasted_iota(jnp.int32, out_ref.shape, 0) // HD
    column = lax.broadcasted_iota(jnp.int32, out_ref.shape, 1) // HD
    out_ref[...] = jnp.where(row == column, 1.0, 0.0).astype(BF16)


def normalised(block, gain):
    values = block.astype(F32)
    centre = values - jnp.mean(values, axis=-1, keepdims=True)
    variance = jnp.mean(centre * centre, axis=-1, keepdims=True)
    return (centre * lax.rsqrt(variance + 1e-05) * gain).astype(BF16)


def head_norm(columns, gain, ones):
    squares = jnp.dot((columns * columns).astype(BF16), ones, preferred_element_type=F32)
    return (columns * lax.rsqrt(squares * (1.0 / HD) + 1e-06) * gain).astype(BF16)


def normalise_kernel(own_ref, sibling_ref, gain_ref, w_ref, out_ref, other_ref):
    for ref, block_ref in ((out_ref, own_ref), (other_ref, sibling_ref)):
        ref[...] = normalised(block_ref[...], gain_ref[...])


def query_kernel(
    own_ref, sibling_ref, w_ref, gains_ref, ones_ref, query_ref, keys_ref, values_ref
):
    rows, width = own_ref.shape
    ones = ones_ref[...]
    spans = [slice(at, at + SPAN) for at in range(0, width, SPAN)]
    projected = [
        (i, span, jnp.dot(ref[...], w_ref[:, span], preferred_element_type=F32))
        for i, ref in enumerate((own_ref, sibling_ref))
        for span in spans
    ]
    for i, span, columns in projected:
        query = head_norm(columns, gains_ref[0:1, span] * SCALE, ones)
        query_ref[span, i * rows : (i + 1) * rows] = query.astype(F32).T.astype(BF16)
    for span in spans:
        columns = [
            jnp.dot(own_ref[...], w_ref[:, at + span.start : at + span.stop], preferred_element_type=F32)
            for at in (width, 2 * width)
        ]
        keys_ref[:, span] = head_norm(columns[0], gains_ref[1:2, span], ones)
        values_ref[span, :] = columns[1].T.astype(BF16)


def pipeline(stages, count):
    for turn in range(count + len(stages) - 1):
        for behind, stage in enumerate(stages):
            if 0 <= turn - behind < count:
                stage(turn - behind)


def absorb(first, made, raws, *refs):
    blocks, refs = refs[: len(raws)], refs[len(raws) :]
    refs_made = [ref[...] for ref in blocks] if made else None
    w_ref, gain_ref, gains_ref, ones_ref, q_ref = refs[:5]
    if first:
        outs = refs[5:]
    else:
        (max_ref, sum_ref, acc_ref), outs = refs[5:8], refs[8:]
        old_max, old_sum = max_ref[...], sum_ref[...]
    width, queries = q_ref.shape
    heads = SPAN // HD
    blocks = [
        normalised(ref[...], gain_ref[...]) if raw else ref[...] for ref, raw in zip(blocks, raws)
    ]
    block = jnp.concatenate(blocks, axis=0) if len(blocks) > 1 and not made else blocks[0]
    if made:
        block, made_values = refs_made
    ones = ones_ref[...]
    zeros = jnp.zeros((HD, queries), BF16)
    counts = jnp.ones((16, block.shape[0]), BF16)
    held = {}
    maxima, sums = [], []

    def project(i):
        if made:
            span = slice(i * SPAN, (i + 1) * SPAN)
            held["key", i], held["value", i] = block[:, span], made_values[span]
            return
        for name, at in (("key", width), ("value", 2 * width)):
            span = slice(at + i * SPAN, at + (i + 1) * SPAN)
            held[name, i] = jnp.dot(block, w_ref[:, span], preferred_element_type=F32)

    def norm(i):
        if made:
            return
        span = slice(i * SPAN, (i + 1) * SPAN)
        held["key", i] = head_norm(held["key", i], gains_ref[1:2, span], ones)
        held["value", i] = held["value", i].T.astype(BF16)

    def score(i):
        keys = held.pop(("key", i))
        for j in range(heads):
            at = i * SPAN + j * HD
            pair = j // 2 * PAIR
            query = q_ref[at : at + HD, :]
            query = jnp.concatenate([query, zeros] if j % 2 == 0 else [zeros, query], axis=0)
            held["score", i, j] = jnp.dot(
                keys[:, pair : pair + PAIR], query, preferred_element_type=F32
            )

    def soften(i):
        scores = [held.pop(("score", i, j)) for j in range(heads)]
        top = jnp.concatenate([jnp.max(s, axis=0, keepdims=True) for s in scores], axis=0)
        if not first:
            before = old_max[i * heads : (i + 1) * heads]
            top = jnp.maximum(top, before)
            held["shrink", i] = jnp.exp2(before - top)
        exponents = [jnp.exp2(s - top[j : j + 1]) for j, s in enumerate(scores)]
        maxima.append(top)
        for j, exponent in enumerate(exponents):
            held["weight", i, j] = exponent.astype(BF16)

    def weigh(i):
        values = held.pop(("value", i))
        for j in range(heads):
            at = i * SPAN + j * HD
            added = jnp.dot(
                jnp.concatenate([values[j * HD : (j + 1) * HD], counts], axis=0),
                held.pop(("weight", i, j)),
                preferred_element_type=F32,
            )
            total, added = added[HD : HD + 1], added[:HD]
            if not first:
                shrink = held["shrink", i][j : j + 1]
                total = total + old_sum[i * heads + j : i * heads + j + 1] * shrink
                added = added + acc_ref[at : at + HD, :] * shrink
            sums.append(total)
            outs[2][at : at + HD, :] = added

    pipeline((project, norm, score, soften, weigh), width // SPAN)
    top, total = jnp.concatenate(maxima, axis=0), jnp.concatenate(sums, axis=0)
    outs[0][...] = top
    outs[1][...] = total


def parted(values):
    high = values.astype(BF16)
    rest = values - high.astype(F32)
    middle = rest.astype(BF16)
    return high, middle, (rest - middle.astype(F32)).astype(BF16)


def half_stages(held, part, q_ref, max_ref, sum_ref, acc_ref, put):
    old_max, old_sum = max_ref[:, part], sum_ref[:, part]
    half = old_max.shape[1]
    zeros = jnp.zeros((HD, half), BF16)
    pairs = [(j, slice(j * PAIR, (j + 1) * PAIR)) for j in range(SPAN // PAIR)]
    maxima, sums = [], []

    def beside(rows, i, j):
        head = (i * SPAN + j * PAIR) // HD
        return jnp.concatenate([rows[head : head + 1], rows[head + 1 : head + 2]], axis=1)

    def score(i):
        keys = held.pop(("key", i))
        for j, pair in pairs:
            at = i * SPAN + j * PAIR
            even, odd = q_ref[at : at + HD, part], q_ref[at + HD : at + PAIR, part]
            query = jnp.concatenate(
                [jnp.concatenate([even, zeros], axis=1), jnp.concatenate([zeros, odd], axis=1)],
                axis=0,
            )
            held["score", i, j] = jnp.dot(keys[:, pair], query, preferred_element_type=F32)

    def soften(i):
        for j, _ in pairs:
            scores, before = held.pop(("score", i, j)), beside(old_max, i, j)
            top = jnp.maximum(jnp.max(scores, axis=0, keepdims=True), before)
            held["shrink", i, j] = jnp.exp2(before - top)
            held["weight", i, j] = jnp.exp2(scores - top).astype(BF16)
            maxima.extend([top[:, :half], top[:, half:]])

    def weigh(i):
        values = held.pop(("value", i))
        counts = jnp.ones((16, values.shape[1]), BF16)
        for j, pair in pairs:
            both = jnp.dot(
                jnp.concatenate([values[pair], counts], axis=0),
                held.pop(("weight", i, j)),
                preferred_element_type=F32,
            )
            shrink = held.pop(("shrink", i, j))
            total = both[PAIR : PAIR + 1] + beside(old_sum, i, j) * shrink
            sums.extend([total[:, :half], total[:, half:]])
            for k, side in enumerate((slice(0, half), slice(half, 2 * half))):
                at = i * SPAN + j * PAIR + k * HD
                added = both[k * HD : (k + 1) * HD, side]
                put(at, added + acc_ref[at : at + HD, part] * shrink[:, side])

    return (score, soften, weigh), maxima, sums


def send_kernel(
    block_ref, w_ref, gain_ref, gains_ref, ones_ref, q_ref, max_ref, sum_ref, acc_ref,
    sent_ref, keys_ref, values_ref,
):
    width, queries = q_ref.shape
    block = normalised(block_ref[...], gain_ref[...])
    ones = ones_ref[...]
    held = {}

    def project(i):
        for name, at in (("key", width), ("value", 2 * width)):
            span = slice(at + i * SPAN, at + (i + 1) * SPAN)
            held[name, i] = jnp.dot(block, w_ref[:, span], preferred_element_type=F32)

    def norm(i):
        span = slice(i * SPAN, (i + 1) * SPAN)
        keys_ref[:, span] = held["key", i] = head_norm(held["key", i], gains_ref[1:2, span], ones)
        values_ref[span, :] = held["value", i] = held["value", i].T.astype(BF16)

    def put(at, rows):
        sent_ref[at : at + HD, :] = rows.astype(BF16)

    part = slice(queries // 2, queries)
    stages, maxima, sums = half_stages(held, part, q_ref, max_ref, sum_ref, acc_ref, put)
    pipeline((project, norm, *stages), width // SPAN)
    top, total = jnp.concatenate(maxima, axis=0), jnp.concatenate(sums, axis=0)
    for i, piece in enumerate((*parted(top), *parted(total))):
        sent_ref[width + i * H : width + (i + 1) * H, :] = piece


def keep_kernel(
    keys_ref, values_ref, q_ref, max_ref, sum_ref, acc_ref, mine_ref, state_ref
):
    width, queries = q_ref.shape
    held = {}
    for i in range(width // SPAN):
        span = slice(i * SPAN, (i + 1) * SPAN)
        held["key", i], held["value", i] = keys_ref[:, span], values_ref[span, :]

    def put(at, rows):
        mine_ref[at : at + HD, :] = rows

    part = slice(0, queries // 2)
    stages, maxima, sums = half_stages(held, part, q_ref, max_ref, sum_ref, acc_ref, put)
    pipeline(stages, width // SPAN)
    state_ref[:H, :] = jnp.concatenate(maxima, axis=0)
    state_ref[H:, :] = jnp.concatenate(sums, axis=0)


def finish_kernel(mine_ref, my_state_ref, theirs_ref, w_ref, out_ref):
    width = mine_ref.shape[0]
    pieces = [theirs_ref[at : at + H, :].astype(F32) for at in range(width, theirs_ref.shape[0], H)]
    their_top, their_total = sum(pieces[1:3], pieces[0]), sum(pieces[4:6], pieces[3])
    top = jnp.maximum(my_state_ref[:H, :], their_top)
    mine, theirs = jnp.exp2(my_state_ref[:H, :] - top), jnp.exp2(their_top - top)
    total = my_state_ref[H:, :] * mine + their_total * theirs
    mine, theirs = mine / total, theirs / total
    spans = []
    for at in range(0, width, SPAN):
        merged = [
            mine_ref[h * HD : (h + 1) * HD, :] * mine[h : h + 1]
            + theirs_ref[h * HD : (h + 1) * HD, :].astype(F32) * theirs[h : h + 1]
            for h in range(at // HD, (at + SPAN) // HD)
        ]
        spans.append(jnp.concatenate(merged, axis=0).T.astype(BF16))
    attended = jnp.concatenate(spans, axis=1)
    out_ref[...] = jnp.dot(attended, w_ref[...], preferred_element_type=F32).astype(BF16)


def call(body, outs, operands, flops, exps=0):
    moved = sum(a.size * a.dtype.itemsize for a in (*operands, *outs))
    return pl.pallas_call(
        body,
        out_shape=outs,
        in_specs=[VMEM] * len(operands),
        out_specs=[VMEM] * len(outs),
        compiler_params=pltpu.CompilerParams(vmem_limit_bytes=24 * 1024 * 1024),
        cost_estimate=pl.CostEstimate(flops=flops, bytes_accessed=moved, transcendentals=exps),
    )(*operands)


def per_device(order, patches, ln_gain, w_qkv, qk_gains, w_out):
    rows, width = patches.shape
    count = lax.axis_size("blk")
    place = {index: i for i, index in enumerate(order)}

    def onward(right_core):
        return [
            (h * count + b, (1 - h) * count + order[(place[b] + step) % count])
            for b in range(count)
            for h, step in ((right_core, 1), (1 - right_core, -1))
        ]

    hops = (onward(1), onward(0))
    axes = ("head", "blk")
    swap = [(0, 1), (1, 0)]

    shape = jax.ShapeDtypeStruct
    tie = lax.optimization_barrier
    (ones,) = call(same_head_kernel, [shape((SPAN, SPAN), BF16)], (), 10_000_000_000)
    one = lax.ppermute(patches, axes, hops[0])
    sibling = lax.ppermute(patches, "head", swap)
    gain = ln_gain.reshape(1, width)
    gain, ones = tie((gain, ones))
    normed, other = call(
        normalise_kernel,
        [shape((rows, width), BF16)] * 2,
        (patches, sibling, gain, w_qkv),
        0,
    )
    two = lax.ppermute(other, axes, hops[0])
    query, keys, values = call(
        query_kernel,
        [shape((width, 2 * rows), BF16), shape((rows, width), BF16), shape((width, rows), BF16)],
        (normed, other, w_qkv, qk_gains, ones),
        2 * 2 * rows * width * width,
    )
    state_shapes = [
        shape((H, 2 * rows), F32),
        shape((H, 2 * rows), F32),
        shape((width, 2 * rows), F32),
    ]
    flops = 2 * rows * width * 2 * width + 2 * 2 * rows * 2 * rows * width

    def take(blocks, state, made=False):
        arrays, raws = zip(*blocks)
        return call(
            functools.partial(absorb, not state, made, raws),
            state_shapes,
            (*arrays, w_qkv, gain, qk_gains, ones, query, *state),
            len(blocks) * flops,
            len(blocks) * H * rows * 2 * rows,
        )

    one, query = tie((one, query))
    own = [(keys, False), (values, False)]
    late, state = None, ()
    for turn in range(1, count // 2):
        here_one, here_two = one, two
        one = lax.ppermute(here_one, axes, hops[turn % 2])
        if turn < count // 2 - 1:
            block = [late] if late else own
            state, here_two = tie((take(block, state, made=not late), here_two))
            two = lax.ppermute(here_two, axes, hops[turn % 2])
            state, one = tie((take([(here_two, False)], state), one))
            late = here_one, True
    state, here_two = tie((take([late, (here_one, True)], state), here_two))
    state, one = tie((take([(here_two, False)], state), one))
    sent, keys, values = call(
        send_kernel,
        [shape((width + 6 * H, rows), BF16), shape((rows, width), BF16), shape((width, rows), BF16)],
        (one, w_qkv, gain, qk_gains, ones, query, *state),
        flops,
        H * rows * rows,
    )
    came = lax.ppermute(sent, "head", swap)
    mine, my_state = call(
        keep_kernel,
        [shape((width, rows), F32), shape((2 * H, rows), F32)],
        (keys, values, query, *state),
        flops // 4,
        H * rows * rows,
    )
    return call(
        finish_kernel,
        [shape((rows, width), BF16)],
        (mine, my_state, came, w_out),
        2 * rows * width * width,
    )[0]


def solution(mesh):
    placed = (P(("group", "head", "blk"), None), P(), P(), P(), P())
    return jax.shard_map(
        functools.partial(per_device, ring_order(mesh)),
        mesh=mesh,
        in_specs=placed,
        out_specs=P(("group", "head", "blk"), None),
        check_vma=False,
    )
```

```python
import functools
import math

import jax
import jax.numpy as jnp
from jax import lax
from jax.experimental import pallas as pl
from jax.experimental.pallas import tpu as pltpu
from jax.sharding import PartitionSpec as P

H = 16
HD = 64
PAIR = 2 * HD
SPAN = 4 * HD
SCALE = HD**-0.5 * math.log2(math.e)
F32 = jnp.float32
BF16 = jnp.bfloat16
VMEM = pl.BlockSpec(memory_space=pltpu.VMEM)


def ring_order(mesh):
    axis = mesh.axis_names.index("blk")
    along = mesh.devices
    for other in reversed(range(along.ndim)):
        if other != axis:
            along = along.take(0, axis=other)
    count = along.shape[0]
    coords = [getattr(device, "coords", None) for device in along]
    if any(c is None for c in coords):
        return list(range(count))
    place = {tuple(c): i for i, c in enumerate(coords)}
    varying = [a for a in range(3) if len({c[a] for c in place}) > 1]
    if len(place) != count or len(varying) != 2:
        return list(range(count))
    short, long = sorted(varying, key=lambda a: len({c[a] for c in place}))
    columns = sorted({c[short] for c in place})
    if len(columns) != 2:
        return list(range(count))
    up = sorted((c for c in place if c[short] == columns[0]), key=lambda c: c[long])
    down = sorted((c for c in place if c[short] == columns[1]), key=lambda c: -c[long])
    return [place[c] for c in up + down]


def same_head_kernel(out_ref):
    row = lax.broadcasted_iota(jnp.int32, out_ref.shape, 0) // HD
    column = lax.broadcasted_iota(jnp.int32, out_ref.shape, 1) // HD
    out_ref[...] = jnp.where(row == column, 1.0, 0.0).astype(BF16)


def normalised(block, gain):
    values = block.astype(F32)
    centre = values - jnp.mean(values, axis=-1, keepdims=True)
    variance = jnp.mean(centre * centre, axis=-1, keepdims=True)
    return (centre * lax.rsqrt(variance + 1e-05) * gain).astype(BF16)


def head_norm(columns, gain, ones):
    squares = jnp.dot((columns * columns).astype(BF16), ones, preferred_element_type=F32)
    return (columns * lax.rsqrt(squares * (1.0 / HD) + 1e-06) * gain).astype(BF16)


def normalise_kernel(own_ref, sibling_ref, gain_ref, w_ref, out_ref, other_ref):
    for ref, block_ref in ((out_ref, own_ref), (other_ref, sibling_ref)):
        ref[...] = normalised(block_ref[...], gain_ref[...])


def query_kernel(
    own_ref, sibling_ref, w_ref, gains_ref, ones_ref, query_ref, keys_ref, values_ref
):
    rows, width = own_ref.shape
    ones = ones_ref[...]
    spans = [slice(at, at + SPAN) for at in range(0, width, SPAN)]
    projected = [
        (i, span, jnp.dot(ref[...], w_ref[:, span], preferred_element_type=F32))
        for i, ref in enumerate((own_ref, sibling_ref))
        for span in spans
    ]
    for i, span, columns in projected:
        query = head_norm(columns, gains_ref[0:1, span] * SCALE, ones)
        query_ref[span, i * rows : (i + 1) * rows] = query.astype(F32).T.astype(BF16)
    for span in spans:
        columns = [
            jnp.dot(own_ref[...], w_ref[:, at + span.start : at + span.stop], preferred_element_type=F32)
            for at in (width, 2 * width)
        ]
        keys_ref[:, span] = head_norm(columns[0], gains_ref[1:2, span], ones)
        values_ref[span, :] = columns[1].T.astype(BF16)


def pipeline(stages, count):
    for turn in range(count + len(stages) - 1):
        for behind, stage in enumerate(stages):
            if 0 <= turn - behind < count:
                stage(turn - behind)


def absorb(first, made, raws, *refs):
    blocks, refs = refs[: len(raws)], refs[len(raws) :]
    refs_made = [ref[...] for ref in blocks] if made else None
    w_ref, gain_ref, gains_ref, ones_ref, q_ref = refs[:5]
    if first:
        outs = refs[5:]
    else:
        (max_ref, sum_ref, acc_ref), outs = refs[5:8], refs[8:]
        old_max, old_sum = max_ref[...], sum_ref[...]
    width, queries = q_ref.shape
    heads = SPAN // HD
    blocks = [
        normalised(ref[...], gain_ref[...]) if raw else ref[...] for ref, raw in zip(blocks, raws)
    ]
    block = jnp.concatenate(blocks, axis=0) if len(blocks) > 1 and not made else blocks[0]
    if made:
        block, made_values = refs_made
    ones = ones_ref[...]
    zeros = jnp.zeros((HD, queries), BF16)
    counts = jnp.ones((16, block.shape[0]), BF16)
    held = {}
    maxima, sums = [], []

    def project(i):
        if made:
            span = slice(i * SPAN, (i + 1) * SPAN)
            held["key", i], held["value", i] = block[:, span], made_values[span]
            return
        for name, at in (("key", width), ("value", 2 * width)):
            span = slice(at + i * SPAN, at + (i + 1) * SPAN)
            held[name, i] = jnp.dot(block, w_ref[:, span], preferred_element_type=F32)

    def norm(i):
        if made:
            return
        span = slice(i * SPAN, (i + 1) * SPAN)
        held["key", i] = head_norm(held["key", i], gains_ref[1:2, span], ones)
        held["value", i] = held["value", i].T.astype(BF16)

    def score(i):
        keys = held.pop(("key", i))
        for j in range(heads):
            at = i * SPAN + j * HD
            pair = j // 2 * PAIR
            query = q_ref[at : at + HD, :]
            query = jnp.concatenate([query, zeros] if j % 2 == 0 else [zeros, query], axis=0)
            held["score", i, j] = jnp.dot(
                keys[:, pair : pair + PAIR], query, preferred_element_type=F32
            )

    def soften(i):
        scores = [held.pop(("score", i, j)) for j in range(heads)]
        top = jnp.concatenate([jnp.max(s, axis=0, keepdims=True) for s in scores], axis=0)
        if not first:
            before = old_max[i * heads : (i + 1) * heads]
            top = jnp.maximum(top, before)
            held["shrink", i] = jnp.exp2(before - top)
        exponents = [jnp.exp2(s - top[j : j + 1]) for j, s in enumerate(scores)]
        maxima.append(top)
        for j, exponent in enumerate(exponents):
            held["weight", i, j] = exponent.astype(BF16)

    def weigh(i):
        values = held.pop(("value", i))
        for j in range(heads):
            at = i * SPAN + j * HD
            added = jnp.dot(
                jnp.concatenate([values[j * HD : (j + 1) * HD], counts], axis=0),
                held.pop(("weight", i, j)),
                preferred_element_type=F32,
            )
            total, added = added[HD : HD + 1], added[:HD]
            if not first:
                shrink = held["shrink", i][j : j + 1]
                total = total + old_sum[i * heads + j : i * heads + j + 1] * shrink
                added = added + acc_ref[at : at + HD, :] * shrink
            sums.append(total)
            outs[2][at : at + HD, :] = added

    pipeline((project, norm, score, soften, weigh), width // SPAN)
    top, total = jnp.concatenate(maxima, axis=0), jnp.concatenate(sums, axis=0)
    outs[0][...] = top
    outs[1][...] = total


def parted(values):
    high = values.astype(BF16)
    rest = values - high.astype(F32)
    middle = rest.astype(BF16)
    return high, middle, (rest - middle.astype(F32)).astype(BF16)


def half_stages(held, part, q_ref, max_ref, sum_ref, acc_ref, put):
    old_max, old_sum = max_ref[:, part], sum_ref[:, part]
    half = old_max.shape[1]
    zeros = jnp.zeros((HD, half), BF16)
    pairs = [(j, slice(j * PAIR, (j + 1) * PAIR)) for j in range(SPAN // PAIR)]
    maxima, sums = [], []

    def beside(rows, i, j):
        head = (i * SPAN + j * PAIR) // HD
        return jnp.concatenate([rows[head : head + 1], rows[head + 1 : head + 2]], axis=1)

    def score(i):
        keys = held.pop(("key", i))
        for j, pair in pairs:
            at = i * SPAN + j * PAIR
            even, odd = q_ref[at : at + HD, part], q_ref[at + HD : at + PAIR, part]
            query = jnp.concatenate(
                [jnp.concatenate([even, zeros], axis=1), jnp.concatenate([zeros, odd], axis=1)],
                axis=0,
            )
            held["score", i, j] = jnp.dot(keys[:, pair], query, preferred_element_type=F32)

    def soften(i):
        for j, _ in pairs:
            scores, before = held.pop(("score", i, j)), beside(old_max, i, j)
            top = jnp.maximum(jnp.max(scores, axis=0, keepdims=True), before)
            held["shrink", i, j] = jnp.exp2(before - top)
            held["weight", i, j] = jnp.exp2(scores - top).astype(BF16)
            maxima.extend([top[:, :half], top[:, half:]])

    def weigh(i):
        values = held.pop(("value", i))
        counts = jnp.ones((16, values.shape[1]), BF16)
        for j, pair in pairs:
            both = jnp.dot(
                jnp.concatenate([values[pair], counts], axis=0),
                held.pop(("weight", i, j)),
                preferred_element_type=F32,
            )
            shrink = held.pop(("shrink", i, j))
            total = both[PAIR : PAIR + 1] + beside(old_sum, i, j) * shrink
            sums.extend([total[:, :half], total[:, half:]])
            for k, side in enumerate((slice(0, half), slice(half, 2 * half))):
                at = i * SPAN + j * PAIR + k * HD
                added = both[k * HD : (k + 1) * HD, side]
                put(at, added + acc_ref[at : at + HD, part] * shrink[:, side])

    return (score, soften, weigh), maxima, sums


def send_kernel(
    block_ref, w_ref, gain_ref, gains_ref, ones_ref, q_ref, max_ref, sum_ref, acc_ref,
    sent_ref, keys_ref, values_ref,
):
    width, queries = q_ref.shape
    block = normalised(block_ref[...], gain_ref[...])
    ones = ones_ref[...]
    held = {}

    def project(i):
        for name, at in (("key", width), ("value", 2 * width)):
            span = slice(at + i * SPAN, at + (i + 1) * SPAN)
            held[name, i] = jnp.dot(block, w_ref[:, span], preferred_element_type=F32)

    def norm(i):
        span = slice(i * SPAN, (i + 1) * SPAN)
        keys_ref[:, span] = held["key", i] = head_norm(held["key", i], gains_ref[1:2, span], ones)
        values_ref[span, :] = held["value", i] = held["value", i].T.astype(BF16)

    def put(at, rows):
        sent_ref[at : at + HD, :] = rows.astype(BF16)

    part = slice(queries // 2, queries)
    stages, maxima, sums = half_stages(held, part, q_ref, max_ref, sum_ref, acc_ref, put)
    pipeline((project, norm, *stages), width // SPAN)
    top, total = jnp.concatenate(maxima, axis=0), jnp.concatenate(sums, axis=0)
    for i, piece in enumerate((*parted(top), *parted(total))):
        sent_ref[width + i * H : width + (i + 1) * H, :] = piece


def keep_kernel(
    keys_ref, values_ref, q_ref, max_ref, sum_ref, acc_ref, mine_ref, state_ref
):
    width, queries = q_ref.shape
    held = {}
    for i in range(width // SPAN):
        span = slice(i * SPAN, (i + 1) * SPAN)
        held["key", i], held["value", i] = keys_ref[:, span], values_ref[span, :]

    def put(at, rows):
        mine_ref[at : at + HD, :] = rows

    part = slice(0, queries // 2)
    stages, maxima, sums = half_stages(held, part, q_ref, max_ref, sum_ref, acc_ref, put)
    pipeline(stages, width // SPAN)
    state_ref[:H, :] = jnp.concatenate(maxima, axis=0)
    state_ref[H:, :] = jnp.concatenate(sums, axis=0)


def finish_kernel(mine_ref, my_state_ref, theirs_ref, w_ref, out_ref):
    width = mine_ref.shape[0]
    pieces = [theirs_ref[at : at + H, :].astype(F32) for at in range(width, theirs_ref.shape[0], H)]
    their_top, their_total = sum(pieces[1:3], pieces[0]), sum(pieces[4:6], pieces[3])
    top = jnp.maximum(my_state_ref[:H, :], their_top)
    mine, theirs = jnp.exp2(my_state_ref[:H, :] - top), jnp.exp2(their_top - top)
    total = my_state_ref[H:, :] * mine + their_total * theirs
    mine, theirs = mine / total, theirs / total
    spans = []
    for at in range(0, width, SPAN):
        merged = [
            mine_ref[h * HD : (h + 1) * HD, :] * mine[h : h + 1]
            + theirs_ref[h * HD : (h + 1) * HD, :].astype(F32) * theirs[h : h + 1]
            for h in range(at // HD, (at + SPAN) // HD)
        ]
        spans.append(jnp.concatenate(merged, axis=0).T.astype(BF16))
    attended = jnp.concatenate(spans, axis=1)
    out_ref[...] = jnp.dot(attended, w_ref[...], preferred_element_type=F32).astype(BF16)


def call(body, outs, operands, flops, exps=0):
    moved = sum(a.size * a.dtype.itemsize for a in (*operands, *outs))
    return pl.pallas_call(
        body,
        out_shape=outs,
        in_specs=[VMEM] * len(operands),
        out_specs=[VMEM] * len(outs),
        compiler_params=pltpu.CompilerParams(vmem_limit_bytes=24 * 1024 * 1024),
        cost_estimate=pl.CostEstimate(flops=flops, bytes_accessed=moved, transcendentals=exps),
    )(*operands)


def per_device(order, patches, ln_gain, w_qkv, qk_gains, w_out):
    rows, width = patches.shape
    count = lax.axis_size("blk")
    place = {index: i for i, index in enumerate(order)}

    def onward(right_core):
        return [
            (h * count + b, (1 - h) * count + order[(place[b] + step) % count])
            for b in range(count)
            for h, step in ((right_core, 1), (1 - right_core, -1))
        ]

    hops = (onward(1), onward(0))
    axes = ("head", "blk")
    swap = [(0, 1), (1, 0)]

    shape = jax.ShapeDtypeStruct
    tie = lax.optimization_barrier
    (ones,) = call(same_head_kernel, [shape((SPAN, SPAN), BF16)], (), 10_000_000_000)
    one = lax.ppermute(patches, axes, hops[0])
    sibling = lax.ppermute(patches, "head", swap)
    gain = ln_gain.reshape(1, width)
    gain, ones = tie((gain, ones))
    normed, other = call(
        normalise_kernel,
        [shape((rows, width), BF16)] * 2,
        (patches, sibling, gain, w_qkv),
        0,
    )
    two = lax.ppermute(other, axes, hops[0])
    query, keys, values = call(
        query_kernel,
        [shape((width, 2 * rows), BF16), shape((rows, width), BF16), shape((width, rows), BF16)],
        (normed, other, w_qkv, qk_gains, ones),
        2 * 2 * rows * width * width,
    )
    state_shapes = [
        shape((H, 2 * rows), F32),
        shape((H, 2 * rows), F32),
        shape((width, 2 * rows), F32),
    ]
    flops = 2 * rows * width * 2 * width + 2 * 2 * rows * 2 * rows * width

    def take(blocks, state, made=False):
        arrays, raws = zip(*blocks)
        return call(
            functools.partial(absorb, not state, made, raws),
            state_shapes,
            (*arrays, w_qkv, gain, qk_gains, ones, query, *state),
            len(blocks) * flops,
            len(blocks) * H * rows * 2 * rows,
        )

    one, query = tie((one, query))
    own = [(keys, False), (values, False)]
    late, state = None, ()
    for turn in range(1, count // 2):
        here_one, here_two = one, two
        one = lax.ppermute(here_one, axes, hops[turn % 2])
        if turn < count // 2 - 1:
            block = [late] if late else own
            state, here_two = tie((take(block, state, made=not late), here_two))
            two = lax.ppermute(here_two, axes, hops[turn % 2])
            state, one = tie((take([(here_one, True)], state), one))
            late = here_two, False
    state, here_two = tie((take([late, (here_one, True)], state), here_two))
    state, one = tie((take([(here_two, False)], state), one))
    sent, keys, values = call(
        send_kernel,
        [shape((width + 6 * H, rows), BF16), shape((rows, width), BF16), shape((width, rows), BF16)],
        (one, w_qkv, gain, qk_gains, ones, query, *state),
        flops,
        H * rows * rows,
    )
    came = lax.ppermute(sent, "head", swap)
    mine, my_state = call(
        keep_kernel,
        [shape((width, rows), F32), shape((2 * H, rows), F32)],
        (keys, values, query, *state),
        flops // 4,
        H * rows * rows,
    )
    return call(
        finish_kernel,
        [shape((rows, width), BF16)],
        (mine, my_state, came, w_out),
        2 * rows * width * width,
    )[0]


def solution(mesh):
    placed = (P(("group", "head", "blk"), None), P(), P(), P(), P())
    return jax.shard_map(
        functools.partial(per_device, ring_order(mesh)),
        mesh=mesh,
        in_specs=placed,
        out_specs=P(("group", "head", "blk"), None),
        check_vma=False,
    )
```
